32 devices in a mesh: parts: 2 (over x), blk: 16 (over z, y, core).
Axes of the slice: x: 2, y: 2, z: 4, core: 2. Of those that a mesh axis runs over, the one named last changes fastest.
Arguments:
- particles: bfloat16 [4096, 4608], P(('parts', 'blk')), parts along dimension 0, may hold values from -24 to 24
- references: bfloat16 [64, 4608], P(('parts', 'blk')), parts along dimension 0, may hold values from -0.5 to 0.5
- inv_noise: float32 [4096], P(('parts', 'blk')), parts along dimension 0, may hold values from 1 to 4
- assign: int32 [4096, 2], P(('parts', 'blk')), parts along dimension 0, may hold values from 0 to 31, all different within a row; in each aligned block of 128 rows (0 to 127, 128 to 255, ...) at most 16 rows name the same one
Outputs:
- class_sums: float32 [64, 4608], P(('parts', 'blk')), parts along dimension 0
- class_mass: float32 [64], P(('parts', 'blk')), parts along dimension 0
- log_evidence: float32 [4096], P(('parts', 'blk')), parts along dimension 0
The draws below stay inside these ranges and needn't reach their ends.
There are 2 independent parts, one for each index of `parts`. The reference program is written for one: setup_inputs(seed, part) draws one part's arguments, and reference() takes and returns one part's arrays. A program takes and returns all parts, laid end to end along the dimension named above; each array names one. Nothing has to cross between parts.
Inputs may be any that keep to these rules, and one draw needn't show every extreme that they name: `assign`: among the rows of one device, at most 16 name any one class; in every draw some device's block reaches this bound.
All inputs are finite; a program needn't handle non-finite values.
Results may differ from the reference program's by a relative error of at most 0.0039.
Values may be sent and summed in bfloat16 or wider, within the bound.
A program may use at most 128 MiB of HBM per device.

```python
import math
import jax
import jax.numpy as jnp
import numpy as np

P_DEV = 128
ROT = 12
TOPK = 2
CYCLES = 12
ANGLES = 384
F = 4608
CLASSES = 32
PARTICLES = 2048
MOST = 16


def class_shapes(key):
    scales = jnp.exp(jax.random.uniform(jax.random.fold_in(key, 11), (CLASSES,), jnp.float32, math.log(0.5), math.log(2.0)))
    normal_part = jnp.clip(jax.random.normal(jax.random.fold_in(key, 12), (CLASSES, F), jnp.float32), -4.0, 4.0)
    shaped = jnp.clip(normal_part * scales[:, None] * F ** (-0.5), -0.5, 0.5)
    return shaped


def draw_references(key, part):
    return class_shapes(key).astype(jnp.bfloat16)


def draw_particles(key, part):
    values = jnp.clip(jax.random.normal(jax.random.fold_in(key, 22), (PARTICLES, F), jnp.float32), -6.0, 6.0)
    values = jnp.clip(values, -24.0, 24.0)
    return values.astype(jnp.bfloat16)


def block_levels(key, extent, pieces, low, high):
    gain = 1.0
    for axis_at, blocks in pieces:
        steps = jax.random.uniform(jax.random.fold_in(jax.random.fold_in(key, 6), axis_at), (blocks,), jnp.float32, low / len(pieces), high / len(pieces))
        gain = gain * jnp.repeat(jnp.exp(steps), extent[axis_at] // blocks).reshape((-1,) + (1,) * (len(extent) - 1 - axis_at))
    return gain


def assign_block(rng, own, number, rows, count, top, most, slope):
    ranking = jax.random.permutation(rng, count)
    heavy_load, common = portions_of(count, rows * top, most, slope, True), portions_of(count, rows * top, most, slope, False)
    places = jnp.arange(count)

    def named(sizes, offset_by):
        used = int((sizes > 0).sum())
        fixed = max(1, used // 4)
        passed = fixed + (places - fixed + offset_by * (used - fixed)) % max(1, count - fixed)
        return jnp.zeros((count,), jnp.int32).at[ranking[jnp.where(places < fixed, places, passed)]].set(jnp.asarray(sizes, jnp.int32))

    sizes = jnp.where(number % 4 == 0, named(heavy_load, number // 4), named(common, number - number // 4 - 1))
    mixed = jax.random.permutation(jax.random.fold_in(own, 3), count)
    donor, receiver = mixed[0:count // 2 * 2:2], mixed[1:count // 2 * 2:2]
    room = jnp.minimum(sizes[donor] - 1, most - sizes[receiver]) // 2
    room = jnp.where((donor == ranking[0]) | (receiver == ranking[0]) | (sizes[receiver] == 0), 0, jnp.maximum(room, 0))
    passed = jax.random.randint(jax.random.fold_in(own, 4), (count // 2,), 0, 1 << 20) % (room + 1)
    sizes = sizes.at[donor].add(-passed).at[receiver].add(passed)
    members = jnp.searchsorted(jnp.cumsum(sizes), jnp.arange(rows * top), side="right").astype(jnp.int32)
    listing = members.reshape(top, rows).T
    listing = listing[jax.random.permutation(jax.random.fold_in(own, 1), rows)]
    offset_by = jax.random.randint(jax.random.fold_in(own, 2), (rows, 1), 0, top)
    return jnp.take_along_axis(listing, (jnp.arange(top)[None, :] + offset_by) % top, axis=1)


def portions_of(count, total, reach, lean, full):
    loads = [(1 << 20) // math.isqrt(rank ** lean) + 1 for rank in range(1, count + 1)]
    largest = reach if full else min(reach, max(-(-total // count), total * loads[0] // sum(loads)))
    least = 1 if total - largest >= count - 1 else 0
    counts, spare = [largest] + [least] * (count - 1), total - largest - least * (count - 1)
    while spare > 0:
        candidates = [i for i in range(1, count) if counts[i] < largest] or [i for i in range(1, count) if counts[i] < reach]
        whole, remaining = sum([loads[i] for i in candidates]), spare
        for i in candidates:
            more = min(reach - counts[i], max(1, remaining * loads[i] // whole), spare)
            counts[i] = counts[i] + more
            spare = spare - more
    return np.array(counts)


def setup_inputs(seed: int = 0, part: int = 0) -> dict:
    key_of = jax.random.split(jax.random.key(seed), 5)
    part_keys = jax.random.split(jax.random.fold_in(key_of[4], part), 5)
    particles = draw_particles(jax.random.fold_in(jax.random.fold_in(key_of[4], part), 71), part)
    references = draw_references(jax.random.fold_in(jax.random.fold_in(key_of[4], part), 71), part)
    inv_noise = jnp.clip(jnp.exp(math.log(4.0) - 1.3862944 * jax.random.uniform(part_keys[2], (PARTICLES,), jnp.float32) ** block_levels(part_keys[2], (PARTICLES,), ((0, 16),), -0.2, 0.2)), 1.0, 4.0)
    assign_keys = jax.random.split(jax.random.fold_in(part_keys[3], 1), PARTICLES // P_DEV)
    assign_turns = jax.random.permutation(jax.random.fold_in(part_keys[3], 3), PARTICLES // P_DEV)
    assign = jax.vmap(lambda own, number: assign_block(jax.random.fold_in(part_keys[3], 2), own, number, P_DEV, CLASSES, TOPK, MOST, 1))(assign_keys, assign_turns).reshape((PARTICLES, TOPK))
    return {"particles": particles, "references": references, "inv_noise": inv_noise, "assign": assign}


def turn_all(cube, sign):
    step = ANGLES // ROT
    return jnp.stack([jnp.roll(cube, sign * r * step, axis=2) for r in range(ROT)], axis=1)


def reference(particles, references, inv_noise, assign):
    cube = references.reshape(CLASSES, CYCLES, ANGLES)
    turned = turn_all(cube, 1).reshape(CLASSES * ROT, F)
    energy = jnp.sum(jnp.square(references.astype(jnp.float32)), axis=1)
    dots = jnp.dot(particles, turned.T, preferred_element_type=jnp.float32)
    logits = inv_noise[:, None] * (dots - 0.5 * jnp.repeat(energy, ROT)[None, :])
    top = jnp.max(logits, axis=1, keepdims=True)
    total = jnp.sum(jnp.exp(logits - top), axis=1, keepdims=True)
    log_evidence = top + jnp.log(total)
    post = jnp.exp(logits - log_evidence).reshape(PARTICLES, CLASSES, ROT)
    picked = jnp.take_along_axis(post, assign[:, :, None].astype(jnp.int32), axis=1)
    pcube = particles.reshape(PARTICLES, CYCLES, ANGLES)
    step = ANGLES // ROT
    rows = jnp.zeros((PARTICLES, TOPK, F), jnp.float32)
    for r in range(ROT):
        back = jnp.roll(pcube, -r * step, axis=2).reshape(PARTICLES, 1, F).astype(jnp.float32)
        rows = rows + picked[:, :, r, None] * back
    rows = rows.astype(jnp.bfloat16).reshape(PARTICLES * TOPK, F)
    weights = jnp.sum(picked, axis=2).astype(jnp.bfloat16).reshape(PARTICLES * TOPK)
    flat = assign.reshape(PARTICLES * TOPK)
    class_sums = jax.ops.segment_sum(rows.astype(jnp.float32), flat, CLASSES)
    class_mass = jax.ops.segment_sum(weights.astype(jnp.float32), flat, CLASSES)
    return class_sums, class_mass, log_evidence[:, 0]
```

```python
import functools

import jax
import jax.numpy as jnp
from jax import lax
from jax.experimental import pallas as pl
from jax.experimental.pallas import tpu as pltpu
from jax.sharding import PartitionSpec as P

ROT = 12
TOPK = 2
CYCLES = 12
ANGLES = 384
STEP = ANGLES // ROT
LANES = 128
TURNS = ANGLES // LANES
SHIFTS = LANES // STEP
MESH = pl.DeviceIdType.MESH


def kernel(n, owned, block_rows, x_hbm, refs_ref, inv_ref, assign_ref, sums_ref, mass_ref, evid_ref,
           x_ref, held, work, part, landed, x_sem, send1, recv1, send2, recv2):
    me = lax.axis_index("blk")
    classes = n * owned
    rows = x_ref.shape[0]

    load = pltpu.make_async_copy(x_hbm, x_ref, x_sem)
    load.start()

    def ahead(d):
        return {"blk": lax.rem(me + d, n)}

    def behind(d):
        return {"blk": lax.rem(me + n - d, n)}

    barrier = pltpu.get_barrier_semaphore()
    for d in range(1, n):
        pl.semaphore_signal(barrier, inc=1, device_id=ahead(d), device_id_type=MESH)

    own = refs_ref[...].astype(jnp.float32)
    for b in range(TURNS):
        work[b, 0:block_rows, :] = jnp.zeros((block_rows, LANES), jnp.float32)
        for c in range(CYCLES):
            at = (c * TURNS + b) * LANES
            work[b, c * owned:(c + 1) * owned, :] = own[:, at:at + LANES]
        held[0, :, b * LANES:(b + 1) * LANES] = work[b, 0:block_rows, :].astype(jnp.bfloat16)

    pl.semaphore_wait(barrier, n - 1)

    gathers = []
    for d in range(1, n):
        copy = pltpu.make_async_remote_copy(
            src_ref=held.at[0], dst_ref=held.at[d], send_sem=send1.at[d], recv_sem=recv1.at[d],
            device_id=ahead(d), device_id_type=MESH)
        copy.start()
        gathers.append(copy)
    load.wait()
    for copy in gathers:
        copy.wait_recv()

    for d in range(n):
        for b in range(TURNS):
            work[b, d * block_rows:(d + 1) * block_rows, :] = held[d, :, b * LANES:(b + 1) * LANES].astype(jnp.float32)

    def shifted(c):
        blocks = [x_ref[:, (c * TURNS + b) * LANES:(c * TURNS + b + 1) * LANES] for b in range(TURNS)]
        return jnp.concatenate(
            [jnp.concatenate([blocks[(b + q) % TURNS] for b in range(TURNS)], axis=1)
             for q in range(TURNS)], axis=0)

    dots = jnp.zeros((SHIFTS * classes, TURNS * rows), jnp.float32)
    energy = jnp.zeros((classes, ANGLES), jnp.float32)
    for c in range(CYCLES):
        ref_c = jnp.concatenate(
            [jnp.concatenate([work[b, pl.ds(c * owned + k, n, stride=block_rows), :] for k in range(owned)], axis=0)
             for b in range(TURNS)], axis=1)
        energy += ref_c * ref_c
        turned = jnp.concatenate(
            [ref_c] + [pltpu.roll(ref_c, s * STEP, 1) for s in range(1, SHIFTS)], axis=0)
        dots += lax.dot_general(
            turned.astype(jnp.bfloat16), shifted(c), (((1,), (1,)), ((), ())),
            preferred_element_type=jnp.float32)

    half = 0.5 * jnp.sum(energy, axis=1, keepdims=True)
    half = jnp.concatenate([half] * SHIFTS, axis=0)
    inv = inv_ref[...]
    logits = jnp.concatenate([inv] * TURNS, axis=1) * (dots - half)

    def across(value, join):
        pieces = [value[:, q * rows:(q + 1) * rows] for q in range(TURNS)]
        return functools.reduce(join, pieces)

    top = across(jnp.max(logits, axis=0, keepdims=True), jnp.maximum)
    scaled = jnp.exp(logits - jnp.concatenate([top] * TURNS, axis=1))
    total = across(jnp.sum(scaled, axis=0, keepdims=True), jnp.add)
    evid_ref[...] = top + jnp.log(total)

    place = lax.broadcasted_iota(jnp.int32, (n, rows), 0)
    source = me - place
    source = jnp.where(source < 0, source + n, source) * owned
    names = jnp.concatenate([source + k for k in range(owned)], axis=0)
    named = names == assign_ref[0:1, :]
    for j in range(1, TOPK):
        named = jnp.logical_or(named, names == assign_ref[j:j + 1, :])
    picked = jnp.where(named, 1.0 / total, 0.0)
    picked = jnp.concatenate([picked] * TURNS, axis=1)
    weight = scaled * jnp.concatenate([picked] * SHIFTS, axis=0)
    mass = jnp.sum(weight, axis=1, keepdims=True)
    mass = functools.reduce(jnp.add, [mass[s * classes:(s + 1) * classes] for s in range(SHIFTS)])
    high = weight.astype(jnp.bfloat16)
    low = (weight - high.astype(jnp.float32)).astype(jnp.bfloat16)
    both = jnp.concatenate([high, low], axis=0)

    def put(row, value):
        for k in range(owned):
            for b in range(TURNS):
                work[b, pl.ds(row * owned + k, n, stride=block_rows), :] = value[k * n:(k + 1) * n, b * LANES:(b + 1) * LANES]

    for c in range(CYCLES):
        mixed = jnp.dot(both, shifted(c), preferred_element_type=jnp.float32)
        out = None
        for s in range(SHIFTS):
            piece = mixed[s * classes:(s + 1) * classes] + mixed[(SHIFTS + s) * classes:(SHIFTS + s + 1) * classes]
            if s:
                piece = pltpu.roll(piece, ANGLES - s * STEP, 1)
            out = piece if out is None else out + piece
        put(c, out)
    mass_high = mass.astype(jnp.bfloat16).astype(jnp.float32)
    lane = lax.broadcasted_iota(jnp.int32, (classes, ANGLES), 1)
    put(CYCLES, jnp.where(lane < LANES, mass_high, mass - mass_high))
    for d in range(n):
        for b in range(TURNS):
            part[d, :, b * LANES:(b + 1) * LANES] = work[b, d * block_rows:(d + 1) * block_rows, :].astype(jnp.bfloat16)

    scatters = []
    for d in range(1, n):
        copy = pltpu.make_async_remote_copy(
            src_ref=part.at[d], dst_ref=landed.at[d], send_sem=send2.at[d], recv_sem=recv2.at[d],
            device_id=behind(d), device_id_type=MESH)
        copy.start()
        scatters.append(copy)
    for copy in gathers:
        copy.wait_send()
    acc = jnp.concatenate([work[b, 0:block_rows, :] for b in range(TURNS)], axis=1)
    for d in range(1, n):
        scatters[d - 1].wait_recv()
        acc = acc + landed[d].astype(jnp.float32)
    for b in range(TURNS):
        work[b, 0:block_rows, :] = acc[:, b * LANES:(b + 1) * LANES]
    for c in range(CYCLES):
        for b in range(TURNS):
            at = (c * TURNS + b) * LANES
            sums_ref[:, at:at + LANES] = work[b, c * owned:(c + 1) * owned, :]
    tail = slice(CYCLES * owned, (CYCLES + 1) * owned)
    mass_ref[...] = work[0, tail, :] + work[1, tail, :]
    for copy in scatters:
        copy.wait_send()


def local(particles, references, inv_noise, assign):
    rows, width = particles.shape
    owned = references.shape[0]
    n = lax.axis_size("blk")
    block_rows = -(-owned * (CYCLES + 1) // 16) * 16
    vmem = pl.BlockSpec(memory_space=pltpu.VMEM)
    sums, mass, evid = pl.pallas_call(
        functools.partial(kernel, n, owned, block_rows),
        out_shape=(
            jax.ShapeDtypeStruct((owned, width), jnp.float32),
            jax.ShapeDtypeStruct((owned, LANES), jnp.float32),
            jax.ShapeDtypeStruct((1, rows), jnp.float32),
        ),
        in_specs=[pl.BlockSpec(memory_space=pl.ANY), vmem, vmem, vmem],
        out_specs=(vmem, vmem, vmem),
        scratch_shapes=[
            pltpu.VMEM((rows, width), jnp.bfloat16),
            pltpu.VMEM((n, block_rows, ANGLES), jnp.bfloat16),
            pltpu.VMEM((TURNS, n * block_rows, LANES), jnp.float32),
            pltpu.VMEM((n, block_rows, ANGLES), jnp.bfloat16),
            pltpu.VMEM((n, block_rows, ANGLES), jnp.bfloat16),
            pltpu.SemaphoreType.DMA,
            pltpu.SemaphoreType.DMA((n,)),
            pltpu.SemaphoreType.DMA((n,)),
            pltpu.SemaphoreType.DMA((n,)),
            pltpu.SemaphoreType.DMA((n,)),
        ],
        compiler_params=pltpu.CompilerParams(
            collective_id=0, has_side_effects=True, vmem_limit_bytes=48 * 1024 * 1024),
        cost_estimate=pl.CostEstimate(
            flops=6 * rows * n * owned * ROT * width, bytes_accessed=2 * rows * width, transcendentals=rows * n * owned * ROT),
    )(particles, references, inv_noise.reshape(1, rows), assign.T)
    return sums, mass[:, 0], evid.reshape(rows)


def solution(mesh):
    placed = (
        P(("parts", "blk"), None),
        P(("parts", "blk"), None),
        P(("parts", "blk")),
        P(("parts", "blk"), None),
    )
    return jax.shard_map(
        local,
        mesh=mesh,
        in_specs=placed,
        out_specs=(P(("parts", "blk"), None), P(("parts", "blk")), P(("parts", "blk"))),
        check_vma=False,
    )
```

```python
import functools

import jax
import jax.numpy as jnp
from jax import lax
from jax.experimental import pallas as pl
from jax.experimental.pallas import tpu as pltpu
from jax.sharding import PartitionSpec as P

ROT = 12
TOPK = 2
CYCLES = 12
ANGLES = 384
STEP = ANGLES // ROT
LANES = 128
TURNS = ANGLES // LANES
SHIFTS = LANES // STEP
DEPTH = 16
MESH = pl.DeviceIdType.MESH


def kernel(n, owned, parts_in, parts_out, x_hbm, refs_hbm, inv_hbm, assign_hbm, sums_ref, mass_ref, evid_ref,
           x_ref, refs_ref, inv_ref, assign_ref, work, *scratch):
    lots = len(parts_in), len(parts_out)
    held, scratch = scratch[:lots[0]], scratch[lots[0]:]
    swap, scratch = scratch[:lots[1]], scratch[lots[1]:]
    swapped, scratch = scratch[:lots[1]], scratch[lots[1]:]
    part, scratch = scratch[:lots[1]], scratch[lots[1]:]
    landed, scratch = scratch[:lots[1]], scratch[lots[1]:]
    x_sem, small_sem, send1, recv1, swap_send, swap_recv, send2, recv2 = scratch
    me = lax.axis_index("blk")
    chips = n // 2
    chip, core = me // 2, lax.rem(me, 2)
    classes = n * owned
    rows = x_ref.shape[0]
    other = {"blk": chip * 2 + 1 - core}

    def ahead(d):
        return {"blk": lax.rem(chip + d, chips) * 2 + core}

    def behind(d):
        return {"blk": lax.rem(chip + chips - d, chips) * 2 + core}

    loads = [pltpu.make_async_copy(src, dst, small_sem.at[i]) for i, (src, dst) in enumerate(
        ((refs_hbm, refs_ref), (inv_hbm, inv_ref), (assign_hbm, assign_ref)))]
    loads.append(pltpu.make_async_copy(x_hbm, x_ref, x_sem))
    for load in loads:
        load.start()

    barrier = pltpu.get_barrier_semaphore()
    pl.semaphore_signal(barrier, inc=1, device_id=other, device_id_type=MESH)
    for d in range(1, chips):
        pl.semaphore_signal(barrier, inc=1, device_id=ahead(d), device_id_type=MESH)

    def spot(c, b, k):
        at = (c * TURNS + b) * owned + k
        return at // DEPTH, at % DEPTH

    loads[0].wait()
    own = refs_ref[...].astype(jnp.float32)
    for j in range(work.shape[0]):
        work[j, 0:DEPTH, :] = jnp.zeros((DEPTH, LANES), jnp.float32)
    for c in range(CYCLES):
        for b in range(TURNS):
            at = (c * TURNS + b) * LANES
            for k in range(owned):
                j, row = spot(c, b, k)
                work[j, row:row + 1, :] = own[k:k + 1, at:at + LANES]

    def each(parts):
        first = 0
        for lot, count in enumerate(parts):
            yield lot, first, count
            first += count

    for lot, first, count in each(parts_in):
        for j in range(count):
            held[lot][0, :, j * LANES:(j + 1) * LANES] = work[first + j, 0:DEPTH, :].astype(jnp.bfloat16)

    pl.semaphore_wait(barrier, chips)

    def move(lot, src, dst, to):
        copy = pltpu.make_async_remote_copy(
            src_ref=held[lot].at[src], dst_ref=held[lot].at[dst], send_sem=send1.at[lot, dst],
            recv_sem=recv1.at[lot, dst], device_id=to, device_id_type=MESH)
        copy.start()
        return copy

    gathers = []
    for lot, _, _ in each(parts_in):
        copies = {d: move(lot, 0, d, ahead(d)) for d in range(1, chips)}
        copies[chips] = move(lot, 0, chips, other)
        gathers.append(copies)
    for load in loads[1:]:
        load.wait()

    def shifted(c):
        blocks = [x_ref[:, (c * TURNS + b) * LANES:(c * TURNS + b + 1) * LANES] for b in range(TURNS)]
        return jnp.concatenate(
            [jnp.concatenate([blocks[(b + q) % TURNS] for b in range(TURNS)], axis=1)
             for q in range(TURNS)], axis=0)

    def spread(lot, first, count):
        copies = gathers[lot]
        for d in range(1, chips):
            copies[d].wait_recv()
            copies[chips + d] = move(lot, d, chips + d, other)
        for d in range(chips):
            copies[chips + d].wait_recv()
        for d in range(n):
            for j in range(count):
                work[first + j, d * DEPTH:(d + 1) * DEPTH, :] = (
                    held[lot][d, :, j * LANES:(j + 1) * LANES].astype(jnp.float32))

    dots = jnp.zeros((SHIFTS * classes, TURNS * rows), jnp.float32)
    energy = jnp.zeros((classes, ANGLES), jnp.float32)
    lots_left = list(each(parts_in))
    ready = 0
    for c in range(CYCLES):
        while ready <= spot(c, TURNS - 1, owned - 1)[0]:
            lot, first, count = lots_left.pop(0)
            spread(lot, first, count)
            ready = first + count
        pieces = []
        for b in range(TURNS):
            column = []
            for k in range(owned):
                j, row = spot(c, b, k)
                column.append(work[j, pl.ds(row, n, stride=DEPTH), :])
            pieces.append(jnp.concatenate(column, axis=0))
        ref_c = jnp.concatenate(pieces, axis=1)
        energy += ref_c * ref_c
        turned = jnp.concatenate(
            [ref_c] + [pltpu.roll(ref_c, s * STEP, 1) for s in range(1, SHIFTS)], axis=0)
        dots += lax.dot_general(
            turned.astype(jnp.bfloat16), shifted(c), (((1,), (1,)), ((), ())),
            preferred_element_type=jnp.float32)

    half = 0.5 * jnp.sum(energy, axis=1, keepdims=True)
    half = jnp.concatenate([half] * SHIFTS, axis=0)
    inv = inv_ref[...]
    logits = jnp.concatenate([inv] * TURNS, axis=1) * (dots - half)

    def across(value, join):
        return functools.reduce(join, [value[:, q * rows:(q + 1) * rows] for q in range(TURNS)])

    top = across(jnp.max(logits, axis=0, keepdims=True), jnp.maximum)
    scaled = jnp.exp(logits - jnp.concatenate([top] * TURNS, axis=1))
    total = across(jnp.sum(scaled, axis=0, keepdims=True), jnp.add)
    evid_ref[...] = top + jnp.log(total)

    slot = lax.broadcasted_iota(jnp.int32, (n, rows), 0)
    side = (slot >= chips).astype(jnp.int32)
    source = chip - (slot - side * chips)
    source = jnp.where(source < 0, source + chips, source) * 2 + jnp.where(side == 0, core, 1 - core)
    names = jnp.concatenate([source * owned + k for k in range(owned)], axis=0)
    named = names == assign_ref[0:1, :]
    for j in range(1, TOPK):
        named = jnp.logical_or(named, names == assign_ref[j:j + 1, :])
    picked = jnp.where(named, 1.0 / total, 0.0)
    picked = jnp.concatenate([picked] * TURNS, axis=1)
    weight = scaled * jnp.concatenate([picked] * SHIFTS, axis=0)
    high = weight.astype(jnp.bfloat16)
    low = (weight - high.astype(jnp.float32)).astype(jnp.bfloat16)
    both = jnp.concatenate([high, low], axis=0)
    mass = jnp.sum(weight, axis=1, keepdims=True)
    mass = functools.reduce(jnp.add, [mass[s * classes:(s + 1) * classes] for s in range(SHIFTS)])

    def put(c, b, value):
        for k in range(owned):
            j, row = spot(c, b, k)
            work[j, pl.ds(row, n, stride=DEPTH), :] = value[k * n:(k + 1) * n]

    mass = jnp.broadcast_to(mass, (classes, LANES))
    mass_high = mass.astype(jnp.bfloat16).astype(jnp.float32)
    lane = lax.broadcasted_iota(jnp.int32, (classes, LANES), 1)
    put(CYCLES, 0, jnp.where(lane < LANES // 2, mass_high, mass - mass_high))

    swaps, scatters = [], []

    def give(lot, first, count):
        for d in range(chips):
            for j in range(count):
                swap[lot][d, :, j * LANES:(j + 1) * LANES] = (
                    work[first + j, (chips + d) * DEPTH:(chips + d + 1) * DEPTH, :].astype(jnp.bfloat16))
        copy = pltpu.make_async_remote_copy(
            src_ref=swap[lot], dst_ref=swapped[lot], send_sem=swap_send.at[lot], recv_sem=swap_recv.at[lot],
            device_id=other, device_id_type=MESH)
        copy.start()
        swaps.append(copy)

    def pass_on(lot, first, count):
        swaps[lot].wait_recv()
        for d in (*range(1, chips), 0):
            for j in range(count):
                both_cores = (work[first + j, d * DEPTH:(d + 1) * DEPTH, :]
                              + swapped[lot][d, :, j * LANES:(j + 1) * LANES].astype(jnp.float32))
                if d:
                    part[lot][d, :, j * LANES:(j + 1) * LANES] = both_cores.astype(jnp.bfloat16)
                else:
                    work[first + j, 0:DEPTH, :] = both_cores
            if d:
                copy = pltpu.make_async_remote_copy(
                    src_ref=part[lot].at[d], dst_ref=landed[lot].at[d], send_sem=send2.at[lot, d],
                    recv_sem=recv2.at[lot, d], device_id=behind(d), device_id_type=MESH)
                copy.start()
                scatters.append((lot, d, first, count, copy))

    lots_left = list(each(parts_out))
    given = []
    for c in range(CYCLES):
        mixed = jnp.dot(both, shifted(c), preferred_element_type=jnp.float32)
        out = None
        for s in range(SHIFTS):
            piece = mixed[s * classes:(s + 1) * classes] + mixed[(SHIFTS + s) * classes:(SHIFTS + s + 1) * classes]
            if s:
                piece = pltpu.roll(piece, ANGLES - s * STEP, 1)
            out = piece if out is None else out + piece
        for b in range(TURNS):
            put(c, b, out[:, b * LANES:(b + 1) * LANES])
        if given and given[0][0] + 3 <= c:
            pass_on(*given.pop(0)[1])
        done = (c + 1) * TURNS * owned
        while lots_left and (done >= (lots_left[0][1] + lots_left[0][2]) * DEPTH or c == CYCLES - 1):
            give(*lots_left[0])
            given.append((c, lots_left.pop(0)))
    for _, lot in given:
        pass_on(*lot)

    for copies in gathers:
        for copy in copies.values():
            copy.wait_send()
    for copy in swaps:
        copy.wait_send()
    for lot, first, count in each(parts_out):
        mine = [one for one in scatters if one[0] == lot]
        acc = [work[first + j, 0:DEPTH, :] for j in range(count)]
        for _, d, _, _, copy in mine:
            copy.wait_recv()
            for j in range(count):
                acc[j] = acc[j] + landed[lot][d, :, j * LANES:(j + 1) * LANES].astype(jnp.float32)
        for j in range(count):
            work[first + j, 0:DEPTH, :] = acc[j]
    for c in range(CYCLES):
        for b in range(TURNS):
            at = (c * TURNS + b) * LANES
            for k in range(owned):
                j, row = spot(c, b, k)
                sums_ref[k:k + 1, at:at + LANES] = work[j, row:row + 1, :]
    for k in range(owned):
        j, row = spot(CYCLES, 0, k)
        tail = work[j, row:row + 1, :]
        mass_ref[k:k + 1, :] = tail + pltpu.roll(tail, LANES // 2, 1)
    for *_, copy in scatters:
        copy.wait_send()


def local(particles, references, inv_noise, assign):
    rows, width = particles.shape
    owned = references.shape[0]
    n = lax.axis_size("blk")
    chips = n // 2
    columns = -(-(CYCLES * TURNS + 1) * owned // DEPTH)
    parts_in = (columns - columns * 2 // 5, columns * 2 // 5)
    parts_out = parts_in[::-1]
    vmem = pl.BlockSpec(memory_space=pltpu.VMEM)
    hbm = pl.BlockSpec(memory_space=pltpu.HBM)

    def slots(count, parts):
        return [pltpu.VMEM((count, DEPTH, part * LANES), jnp.bfloat16) for part in parts]

    sums, mass, evid = pl.pallas_call(
        functools.partial(kernel, n, owned, parts_in, parts_out),
        out_shape=(
            jax.ShapeDtypeStruct((owned, width), jnp.float32),
            jax.ShapeDtypeStruct((owned, LANES), jnp.float32),
            jax.ShapeDtypeStruct((1, rows), jnp.float32),
        ),
        in_specs=[hbm] * 4,
        out_specs=(vmem, vmem, vmem),
        scratch_shapes=[
            pltpu.VMEM((rows, width), jnp.bfloat16),
            pltpu.VMEM((owned, width), jnp.bfloat16),
            pltpu.VMEM((1, rows), jnp.float32),
            pltpu.VMEM((TOPK, rows), jnp.int32),
            pltpu.VMEM((columns, n * DEPTH, LANES), jnp.float32),
            *slots(n, parts_in),
            *slots(chips, parts_out),
            *slots(chips, parts_out),
            *slots(chips, parts_out),
            *slots(chips, parts_out),
            pltpu.SemaphoreType.DMA,
            pltpu.SemaphoreType.DMA((3,)),
            pltpu.SemaphoreType.DMA((2, n)),
            pltpu.SemaphoreType.DMA((2, n)),
            pltpu.SemaphoreType.DMA((2,)),
            pltpu.SemaphoreType.DMA((2,)),
            pltpu.SemaphoreType.DMA((2, chips)),
            pltpu.SemaphoreType.DMA((2, chips)),
        ],
        compiler_params=pltpu.CompilerParams(
            collective_id=0, has_side_effects=True, vmem_limit_bytes=48 * 1024 * 1024),
        cost_estimate=pl.CostEstimate(
            flops=6 * rows * n * owned * ROT * width, bytes_accessed=2 * rows * width, transcendentals=rows * n * owned * ROT),
    )(particles, references, inv_noise.reshape(1, rows), assign.T)
    return sums, mass[:, 0], evid.reshape(rows)


def solution(mesh):
    placed = (
        P(("parts", "blk"), None),
        P(("parts", "blk"), None),
        P(("parts", "blk")),
        P(("parts", "blk"), None),
    )
    return jax.shard_map(
        local,
        mesh=mesh,
        in_specs=placed,
        out_specs=(P(("parts", "blk"), None), P(("parts", "blk")), P(("parts", "blk"))),
        check_vma=False,
    )
```

```python
import functools

import jax
import jax.numpy as jnp
from jax import lax
from jax.experimental import pallas as pl
from jax.experimental.pallas import tpu as pltpu
from jax.sharding import PartitionSpec as P

ROT = 12
TOPK = 2
CYCLES = 12
ANGLES = 384
STEP = ANGLES // ROT
LANES = 128
TURNS = ANGLES // LANES
SHIFTS = LANES // STEP
DEPTH = 16
MESH = pl.DeviceIdType.MESH


def kernel(n, owned, parts_in, parts_out, x_hbm, refs_hbm, inv_hbm, assign_hbm, sums_ref, mass_ref, evid_ref,
           x_ref, xt_ref, refs_ref, inv_ref, assign_ref, work, *scratch):
    lots = len(parts_in), len(parts_out)
    held, scratch = scratch[:lots[0]], scratch[lots[0]:]
    swap, scratch = scratch[:lots[1]], scratch[lots[1]:]
    swapped, scratch = scratch[:lots[1]], scratch[lots[1]:]
    part, scratch = scratch[:lots[1]], scratch[lots[1]:]
    landed, scratch = scratch[:lots[1]], scratch[lots[1]:]
    x_sem, small_sem, send1, recv1, swap_send, swap_recv, send2, recv2 = scratch
    me = lax.axis_index("blk")
    chips = n // 2
    chip, core = me // 2, lax.rem(me, 2)
    classes = n * owned
    rows = x_ref.shape[0]
    other = {"blk": chip * 2 + 1 - core}

    def ahead(d):
        return {"blk": lax.rem(chip + d, chips) * 2 + core}

    def behind(d):
        return {"blk": lax.rem(chip + chips - d, chips) * 2 + core}

    loads = [pltpu.make_async_copy(src, dst, small_sem.at[i]) for i, (src, dst) in enumerate(
        ((refs_hbm, refs_ref), (inv_hbm, inv_ref), (assign_hbm, assign_ref)))]
    loads.append(pltpu.make_async_copy(x_hbm, x_ref, x_sem))
    for load in loads:
        load.start()

    barrier = pltpu.get_barrier_semaphore()
    pl.semaphore_signal(barrier, inc=1, device_id=other, device_id_type=MESH)
    for d in range(1, chips):
        pl.semaphore_signal(barrier, inc=1, device_id=ahead(d), device_id_type=MESH)

    def spot(c, b, k):
        at = (c * TURNS + b) * owned + k
        return at // DEPTH, at % DEPTH

    loads[0].wait()
    own = refs_ref[...].astype(jnp.float32)
    for j in range(work.shape[0]):
        work[j, 0:DEPTH, :] = jnp.zeros((DEPTH, LANES), jnp.float32)
    for c in range(CYCLES):
        for b in range(TURNS):
            at = (c * TURNS + b) * LANES
            for k in range(owned):
                j, row = spot(c, b, k)
                work[j, row:row + 1, :] = own[k:k + 1, at:at + LANES]

    def each(parts):
        first = 0
        for lot, count in enumerate(parts):
            yield lot, first, count
            first += count

    for lot, first, count in each(parts_in):
        for j in range(count):
            held[lot][0, :, j * LANES:(j + 1) * LANES] = work[first + j, 0:DEPTH, :].astype(jnp.bfloat16)

    pl.semaphore_wait(barrier, chips)

    def move(lot, src, dst, to):
        copy = pltpu.make_async_remote_copy(
            src_ref=held[lot].at[src], dst_ref=held[lot].at[dst], send_sem=send1.at[lot, dst],
            recv_sem=recv1.at[lot, dst], device_id=to, device_id_type=MESH)
        copy.start()
        return copy

    gathers = []
    for lot, _, _ in each(parts_in):
        copies = {d: move(lot, 0, d, ahead(d)) for d in range(1, chips)}
        copies[chips] = move(lot, 0, chips, other)
        gathers.append(copies)
    for load in loads[1:]:
        load.wait()
    for at in range(0, x_ref.shape[1], LANES):
        xt_ref[at:at + LANES, :] = x_ref[:, at:at + LANES].T

    def shifted(c):
        blocks = [x_ref[:, (c * TURNS + b) * LANES:(c * TURNS + b + 1) * LANES] for b in range(TURNS)]
        return jnp.concatenate(
            [jnp.concatenate([blocks[(b + q) % TURNS] for b in range(TURNS)], axis=1)
             for q in range(TURNS)], axis=0)

    def spread(lot, first, count):
        copies = gathers[lot]
        for d in range(1, chips):
            copies[d].wait_recv()
            copies[chips + d] = move(lot, d, chips + d, other)
        for d in range(chips):
            copies[chips + d].wait_recv()
        for d in range(n):
            for j in range(count):
                work[first + j, d * DEPTH:(d + 1) * DEPTH, :] = (
                    held[lot][d, :, j * LANES:(j + 1) * LANES].astype(jnp.float32))

    dots = jnp.zeros((ROT * classes, rows), jnp.float32)
    energy = jnp.zeros((classes, ANGLES), jnp.float32)
    turned = []
    lots_left = list(each(parts_in))
    ready = 0
    for c in range(CYCLES):
        while ready <= spot(c, TURNS - 1, owned - 1)[0]:
            lot, first, count = lots_left.pop(0)
            spread(lot, first, count)
            ready = first + count
        pieces = []
        for b in range(TURNS):
            column = []
            for k in range(owned):
                j, row = spot(c, b, k)
                column.append(work[j, pl.ds(row, n, stride=DEPTH), :])
            pieces.append(jnp.concatenate(column, axis=0))
        ref_c = jnp.concatenate(pieces, axis=1)
        energy += ref_c * ref_c
        shifts = jnp.concatenate(
            [ref_c] + [pltpu.roll(ref_c, s * STEP, 1) for s in range(1, SHIFTS)], axis=0).astype(jnp.bfloat16)
        blocks = [shifts[:, b * LANES:(b + 1) * LANES] for b in range(TURNS)]
        turned.append(jnp.concatenate(
            [jnp.concatenate([blocks[(b - q) % TURNS] for b in range(TURNS)], axis=1)
             for q in range(TURNS)], axis=0))
        if len(turned) == 2:
            dots += jnp.dot(
                jnp.concatenate(turned, axis=1), xt_ref[(c - 1) * ANGLES:(c + 1) * ANGLES, :],
                preferred_element_type=jnp.float32)
            turned = []

    half = 0.5 * jnp.sum(energy, axis=1, keepdims=True)
    logits = inv_ref[...] * (dots - jnp.concatenate([half] * ROT, axis=0))
    top = jnp.max(logits, axis=0, keepdims=True)
    scaled = jnp.exp(logits - top)
    total = jnp.sum(scaled, axis=0, keepdims=True)
    evid_ref[...] = top + jnp.log(total)

    slot = lax.broadcasted_iota(jnp.int32, (n, rows), 0)
    side = (slot >= chips).astype(jnp.int32)
    source = chip - (slot - side * chips)
    source = jnp.where(source < 0, source + chips, source) * 2 + jnp.where(side == 0, core, 1 - core)
    names = jnp.concatenate([source * owned + k for k in range(owned)], axis=0)
    named = names == assign_ref[0:1, :]
    for j in range(1, TOPK):
        named = jnp.logical_or(named, names == assign_ref[j:j + 1, :])
    picked = jnp.where(named, 1.0 / total, 0.0)
    weight = scaled * jnp.concatenate([picked] * ROT, axis=0)
    mass = functools.reduce(jnp.add, [weight[r * classes:(r + 1) * classes] for r in range(ROT)])
    mass = jnp.sum(mass, axis=1, keepdims=True)
    turn = SHIFTS * classes
    weight = jnp.concatenate([weight[q * turn:(q + 1) * turn] for q in range(TURNS)], axis=1)
    high = weight.astype(jnp.bfloat16)
    low = (weight - high.astype(jnp.float32)).astype(jnp.bfloat16)
    both = jnp.concatenate([high, low], axis=0)

    def put(c, b, value):
        for k in range(owned):
            j, row = spot(c, b, k)
            work[j, pl.ds(row, n, stride=DEPTH), :] = value[k * n:(k + 1) * n]

    mass = jnp.broadcast_to(mass, (classes, LANES))
    mass_high = mass.astype(jnp.bfloat16).astype(jnp.float32)
    lane = lax.broadcasted_iota(jnp.int32, (classes, LANES), 1)
    put(CYCLES, 0, jnp.where(lane < LANES // 2, mass_high, mass - mass_high))

    swaps, scatters = [], []

    def give(lot, first, count):
        for d in range(chips):
            for j in range(count):
                swap[lot][d, :, j * LANES:(j + 1) * LANES] = (
                    work[first + j, (chips + d) * DEPTH:(chips + d + 1) * DEPTH, :].astype(jnp.bfloat16))
        copy = pltpu.make_async_remote_copy(
            src_ref=swap[lot], dst_ref=swapped[lot], send_sem=swap_send.at[lot], recv_sem=swap_recv.at[lot],
            device_id=other, device_id_type=MESH)
        copy.start()
        swaps.append(copy)

    def pass_on(lot, first, count):
        swaps[lot].wait_recv()
        for d in (*range(1, chips), 0):
            for j in range(count):
                both_cores = (work[first + j, d * DEPTH:(d + 1) * DEPTH, :]
                              + swapped[lot][d, :, j * LANES:(j + 1) * LANES].astype(jnp.float32))
                if d:
                    part[lot][d, :, j * LANES:(j + 1) * LANES] = both_cores.astype(jnp.bfloat16)
                else:
                    work[first + j, 0:DEPTH, :] = both_cores
            if d:
                copy = pltpu.make_async_remote_copy(
                    src_ref=part[lot].at[d], dst_ref=landed[lot].at[d], send_sem=send2.at[lot, d],
                    recv_sem=recv2.at[lot, d], device_id=behind(d), device_id_type=MESH)
                copy.start()
                scatters.append((lot, d, first, count, copy))

    lots_left = list(each(parts_out))
    given = []
    for c in range(CYCLES):
        mixed = jnp.dot(both, shifted(c), preferred_element_type=jnp.float32)
        out = None
        for s in range(SHIFTS):
            piece = mixed[s * classes:(s + 1) * classes] + mixed[(SHIFTS + s) * classes:(SHIFTS + s + 1) * classes]
            if s:
                piece = pltpu.roll(piece, ANGLES - s * STEP, 1)
            out = piece if out is None else out + piece
        for b in range(TURNS):
            put(c, b, out[:, b * LANES:(b + 1) * LANES])
        if given and given[0][0] + 3 <= c:
            pass_on(*given.pop(0)[1])
        done = (c + 1) * TURNS * owned
        while lots_left and (done >= (lots_left[0][1] + lots_left[0][2]) * DEPTH or c == CYCLES - 1):
            give(*lots_left[0])
            given.append((c, lots_left.pop(0)))
    for _, lot in given:
        pass_on(*lot)

    for copies in gathers:
        for copy in copies.values():
            copy.wait_send()
    for copy in swaps:
        copy.wait_send()
    for lot, first, count in each(parts_out):
        mine = [one for one in scatters if one[0] == lot]
        acc = [work[first + j, 0:DEPTH, :] for j in range(count)]
        for _, d, _, _, copy in mine:
            copy.wait_recv()
            for j in range(count):
                acc[j] = acc[j] + landed[lot][d, :, j * LANES:(j + 1) * LANES].astype(jnp.float32)
        for j in range(count):
            work[first + j, 0:DEPTH, :] = acc[j]
    for c in range(CYCLES):
        for b in range(TURNS):
            at = (c * TURNS + b) * LANES
            for k in range(owned):
                j, row = spot(c, b, k)
                sums_ref[k:k + 1, at:at + LANES] = work[j, row:row + 1, :]
    for k in range(owned):
        j, row = spot(CYCLES, 0, k)
        tail = work[j, row:row + 1, :]
        mass_ref[k:k + 1, :] = tail + pltpu.roll(tail, LANES // 2, 1)
    for *_, copy in scatters:
        copy.wait_send()


def local(particles, references, inv_noise, assign):
    rows, width = particles.shape
    owned = references.shape[0]
    n = lax.axis_size("blk")
    chips = n // 2
    columns = -(-(CYCLES * TURNS + 1) * owned // DEPTH)
    parts_in = (columns - columns * 2 // 5, columns * 2 // 5)
    parts_out = parts_in[::-1]
    vmem = pl.BlockSpec(memory_space=pltpu.VMEM)
    hbm = pl.BlockSpec(memory_space=pltpu.HBM)

    def slots(count, parts):
        return [pltpu.VMEM((count, DEPTH, part * LANES), jnp.bfloat16) for part in parts]

    sums, mass, evid = pl.pallas_call(
        functools.partial(kernel, n, owned, parts_in, parts_out),
        out_shape=(
            jax.ShapeDtypeStruct((owned, width), jnp.float32),
            jax.ShapeDtypeStruct((owned, LANES), jnp.float32),
            jax.ShapeDtypeStruct((1, rows), jnp.float32),
        ),
        in_specs=[hbm] * 4,
        out_specs=(vmem, vmem, vmem),
        scratch_shapes=[
            pltpu.VMEM((rows, width), jnp.bfloat16),
            pltpu.VMEM((width, rows), jnp.bfloat16),
            pltpu.VMEM((owned, width), jnp.bfloat16),
            pltpu.VMEM((1, rows), jnp.float32),
            pltpu.VMEM((TOPK, rows), jnp.int32),
            pltpu.VMEM((columns, n * DEPTH, LANES), jnp.float32),
            *slots(n, parts_in),
            *slots(chips, parts_out),
            *slots(chips, parts_out),
            *slots(chips, parts_out),
            *slots(chips, parts_out),
            pltpu.SemaphoreType.DMA,
            pltpu.SemaphoreType.DMA((3,)),
            pltpu.SemaphoreType.DMA((2, n)),
            pltpu.SemaphoreType.DMA((2, n)),
            pltpu.SemaphoreType.DMA((2,)),
            pltpu.SemaphoreType.DMA((2,)),
            pltpu.SemaphoreType.DMA((2, chips)),
            pltpu.SemaphoreType.DMA((2, chips)),
        ],
        compiler_params=pltpu.CompilerParams(
            collective_id=0, has_side_effects=True, vmem_limit_bytes=64 * 1024 * 1024 - 65536),
        cost_estimate=pl.CostEstimate(
            flops=6 * rows * n * owned * ROT * width, bytes_accessed=2 * rows * width, transcendentals=rows * n * owned * ROT),
    )(particles, references, inv_noise.reshape(1, rows), assign.T)
    return sums, mass[:, 0], evid.reshape(rows)


def solution(mesh):
    placed = (
        P(("parts", "blk"), None),
        P(("parts", "blk"), None),
        P(("parts", "blk")),
        P(("parts", "blk"), None),
    )
    return jax.shard_map(
        local,
        mesh=mesh,
        in_specs=placed,
        out_specs=(P(("parts", "blk"), None), P(("parts", "blk")), P(("parts", "blk"))),
        check_vma=False,
    )
```

```python
import functools

import jax
import jax.numpy as jnp
from jax import lax
from jax.experimental import pallas as pl
from jax.experimental.pallas import tpu as pltpu
from jax.sharding import PartitionSpec as P

ROT = 12
TOPK = 2
CYCLES = 12
ANGLES = 384
STEP = ANGLES // ROT
LANES = 128
TURNS = ANGLES // LANES
SHIFTS = LANES // STEP
DEPTH = 16
MESH = pl.DeviceIdType.MESH


def spot(owned, c, b, k):
    at = (c * TURNS + b) * owned + k
    return at // DEPTH, at % DEPTH


def each(parts):
    first = 0
    for lot, count in enumerate(parts):
        yield lot, first, count
        first += count


def kernel(n, owned, parts_in, parts_out, x_hbm, refs_hbm, inv_hbm, assign_hbm, *scratch):
    lots = len(parts_in), len(parts_out)
    landed, scratch = scratch[:lots[1]], scratch[lots[1]:]
    own_hbm, evid_hbm, x_ref, xt_ref, refs_ref, inv_ref, assign_ref, evid_ref, work = scratch[:9]
    scratch = scratch[9:]
    held, scratch = scratch[:lots[0]], scratch[lots[0]:]
    swap, scratch = scratch[:lots[1]], scratch[lots[1]:]
    swapped, scratch = scratch[:lots[1]], scratch[lots[1]:]
    part, scratch = scratch[:lots[1]], scratch[lots[1]:]
    x_sem, small_sem, own_sem, evid_sem, send1, recv1, swap_send, swap_recv, send2, recv2 = scratch
    me = lax.axis_index("blk")
    chips = n // 2
    chip, core = me // 2, lax.rem(me, 2)
    classes = n * owned
    rows = x_ref.shape[0]
    other = {"blk": chip * 2 + 1 - core}

    def ahead(d):
        return {"blk": lax.rem(chip + d, chips) * 2 + core}

    def behind(d):
        return {"blk": lax.rem(chip + chips - d, chips) * 2 + core}

    loads = [pltpu.make_async_copy(src, dst, small_sem.at[i]) for i, (src, dst) in enumerate(
        ((refs_hbm, refs_ref), (inv_hbm, inv_ref), (assign_hbm, assign_ref)))]
    loads.append(pltpu.make_async_copy(x_hbm, x_ref, x_sem))
    for load in loads:
        load.start()

    barrier = pltpu.get_barrier_semaphore()
    pl.semaphore_signal(barrier, inc=1, device_id=other, device_id_type=MESH)
    for d in range(1, chips):
        pl.semaphore_signal(barrier, inc=1, device_id=ahead(d), device_id_type=MESH)

    loads[0].wait()
    own = refs_ref[...].astype(jnp.float32)
    for j in range(work.shape[0]):
        work[j, 0:DEPTH, :] = jnp.zeros((DEPTH, LANES), jnp.float32)
    for c in range(CYCLES):
        for b in range(TURNS):
            at = (c * TURNS + b) * LANES
            for k in range(owned):
                j, row = spot(owned, c, b, k)
                work[j, row:row + 1, :] = own[k:k + 1, at:at + LANES]

    for lot, first, count in each(parts_in):
        for j in range(count):
            held[lot][0, :, j * LANES:(j + 1) * LANES] = work[first + j, 0:DEPTH, :].astype(jnp.bfloat16)

    pl.semaphore_wait(barrier, chips)

    def move(lot, src, dst, to):
        copy = pltpu.make_async_remote_copy(
            src_ref=held[lot].at[src], dst_ref=held[lot].at[dst], send_sem=send1.at[lot, dst],
            recv_sem=recv1.at[lot, dst], device_id=to, device_id_type=MESH)
        copy.start()
        return copy

    gathers = []
    for lot, _, _ in each(parts_in):
        copies = {d: move(lot, 0, d, ahead(d)) for d in range(1, chips)}
        copies[chips] = move(lot, 0, chips, other)
        gathers.append(copies)
    for load in loads[1:]:
        load.wait()
    for at in range(0, x_ref.shape[1], LANES):
        xt_ref[at:at + LANES, :] = x_ref[:, at:at + LANES].T

    def shifted(c):
        blocks = [x_ref[:, (c * TURNS + b) * LANES:(c * TURNS + b + 1) * LANES] for b in range(TURNS)]
        return jnp.concatenate(
            [jnp.concatenate([blocks[(b + q) % TURNS] for b in range(TURNS)], axis=1)
             for q in range(TURNS)], axis=0)

    def spread(lot, first, count):
        copies = gathers[lot]
        for d in range(1, chips):
            copies[d].wait_recv()
            copies[chips + d] = move(lot, d, chips + d, other)
        for d in range(chips):
            copies[chips + d].wait_recv()
        for d in range(n):
            for j in range(count):
                work[first + j, d * DEPTH:(d + 1) * DEPTH, :] = (
                    held[lot][d, :, j * LANES:(j + 1) * LANES].astype(jnp.float32))

    dots = jnp.zeros((ROT * classes, rows), jnp.float32)
    energy = jnp.zeros((classes, ANGLES), jnp.float32)
    turned = []
    lots_left = list(each(parts_in))
    ready = 0
    for c in range(CYCLES):
        while ready <= spot(owned, c, TURNS - 1, owned - 1)[0]:
            lot, first, count = lots_left.pop(0)
            spread(lot, first, count)
            ready = first + count
        pieces = []
        for b in range(TURNS):
            column = []
            for k in range(owned):
                j, row = spot(owned, c, b, k)
                column.append(work[j, pl.ds(row, n, stride=DEPTH), :])
            pieces.append(jnp.concatenate(column, axis=0))
        ref_c = jnp.concatenate(pieces, axis=1)
        energy += ref_c * ref_c
        shifts = jnp.concatenate(
            [ref_c] + [pltpu.roll(ref_c, s * STEP, 1) for s in range(1, SHIFTS)], axis=0).astype(jnp.bfloat16)
        blocks = [shifts[:, b * LANES:(b + 1) * LANES] for b in range(TURNS)]
        turned.append(jnp.concatenate(
            [jnp.concatenate([blocks[(b - q) % TURNS] for b in range(TURNS)], axis=1)
             for q in range(TURNS)], axis=0))
        if len(turned) == 2:
            dots += jnp.dot(
                jnp.concatenate(turned, axis=1), xt_ref[(c - 1) * ANGLES:(c + 1) * ANGLES, :],
                preferred_element_type=jnp.float32)
            turned = []

    half = 0.5 * jnp.sum(energy, axis=1, keepdims=True)
    logits = inv_ref[...] * (dots - jnp.concatenate([half] * ROT, axis=0))
    top = jnp.max(logits, axis=0, keepdims=True)
    scaled = jnp.exp(logits - top)
    total = jnp.sum(scaled, axis=0, keepdims=True)
    evid_ref[...] = top + jnp.log(total)
    evid_copy = pltpu.make_async_copy(evid_ref, evid_hbm, evid_sem)
    evid_copy.start()

    slot = lax.broadcasted_iota(jnp.int32, (n, rows), 0)
    side = (slot >= chips).astype(jnp.int32)
    source = chip - (slot - side * chips)
    source = jnp.where(source < 0, source + chips, source) * 2 + jnp.where(side == 0, core, 1 - core)
    names = jnp.concatenate([source * owned + k for k in range(owned)], axis=0)
    named = names == assign_ref[0:1, :]
    for j in range(1, TOPK):
        named = jnp.logical_or(named, names == assign_ref[j:j + 1, :])
    picked = jnp.where(named, 1.0 / total, 0.0)
    weight = scaled * jnp.concatenate([picked] * ROT, axis=0)
    mass = functools.reduce(jnp.add, [weight[r * classes:(r + 1) * classes] for r in range(ROT)])
    mass = jnp.sum(mass, axis=1, keepdims=True)
    turn = SHIFTS * classes
    weight = jnp.concatenate([weight[q * turn:(q + 1) * turn] for q in range(TURNS)], axis=1)
    high = weight.astype(jnp.bfloat16)
    low = (weight - high.astype(jnp.float32)).astype(jnp.bfloat16)
    both = jnp.concatenate([high, low], axis=0)

    def put(c, b, value):
        for k in range(owned):
            j, row = spot(owned, c, b, k)
            work[j, pl.ds(row, n, stride=DEPTH), :] = value[k * n:(k + 1) * n]

    mass = jnp.broadcast_to(mass, (classes, LANES))
    mass_high = mass.astype(jnp.bfloat16).astype(jnp.float32)
    lane = lax.broadcasted_iota(jnp.int32, (classes, LANES), 1)
    put(CYCLES, 0, jnp.where(lane < LANES // 2, mass_high, mass - mass_high))

    swaps, scatters, own_copies = [], [], []

    def give(lot, first, count):
        for d in range(chips):
            for j in range(count):
                swap[lot][d, :, j * LANES:(j + 1) * LANES] = (
                    work[first + j, (chips + d) * DEPTH:(chips + d + 1) * DEPTH, :].astype(jnp.bfloat16))
        copy = pltpu.make_async_remote_copy(
            src_ref=swap[lot], dst_ref=swapped[lot], send_sem=swap_send.at[lot], recv_sem=swap_recv.at[lot],
            device_id=other, device_id_type=MESH)
        copy.start()
        swaps.append(copy)

    def pass_on(lot, first, count):
        swaps[lot].wait_recv()
        for d in (*range(1, chips), 0):
            for j in range(count):
                both_cores = (work[first + j, d * DEPTH:(d + 1) * DEPTH, :]
                              + swapped[lot][d, :, j * LANES:(j + 1) * LANES].astype(jnp.float32))
                if d:
                    part[lot][d, :, j * LANES:(j + 1) * LANES] = both_cores.astype(jnp.bfloat16)
                else:
                    work[first + j, 0:DEPTH, :] = both_cores
            if d:
                copy = pltpu.make_async_remote_copy(
                    src_ref=part[lot].at[d], dst_ref=landed[lot].at[d], send_sem=send2.at[lot, d],
                    recv_sem=recv2.at[lot, d], device_id=behind(d), device_id_type=MESH)
                copy.start()
                scatters.append(copy)
        copy = pltpu.make_async_copy(
            work.at[first:first + count, 0:DEPTH], own_hbm.at[first:first + count], own_sem.at[lot])
        copy.start()
        own_copies.append(copy)

    lots_left = list(each(parts_out))
    given = []
    for c in range(CYCLES):
        mixed = jnp.dot(both, shifted(c), preferred_element_type=jnp.float32)
        out = None
        for s in range(SHIFTS):
            piece = mixed[s * classes:(s + 1) * classes] + mixed[(SHIFTS + s) * classes:(SHIFTS + s + 1) * classes]
            if s:
                piece = pltpu.roll(piece, ANGLES - s * STEP, 1)
            out = piece if out is None else out + piece
        for b in range(TURNS):
            put(c, b, out[:, b * LANES:(b + 1) * LANES])
        if given and given[0][0] + 3 <= c:
            pass_on(*given.pop(0)[1])
        done = (c + 1) * TURNS * owned
        while lots_left and (done >= (lots_left[0][1] + lots_left[0][2]) * DEPTH or c == CYCLES - 1):
            give(*lots_left[0])
            given.append((c, lots_left.pop(0)))
    for _, lot in given:
        pass_on(*lot)

    for copies in gathers:
        for copy in copies.values():
            copy.wait_send()
    for copy in swaps:
        copy.wait_send()
    for copy in own_copies:
        copy.wait()
    evid_copy.wait()
    for copy in scatters:
        copy.wait()


def finish(owned, parts_out, *refs):
    lots = len(parts_out)
    landed, (own_hbm, evid_hbm, sums_ref, mass_ref, evid_ref) = refs[:lots], refs[lots:lots + 5]
    arrived, (work, evid, sems) = refs[lots + 5:-3], refs[-3:]
    loads = [pltpu.make_async_copy(src, dst, sems.at[i]) for i, (src, dst) in enumerate(
        zip((own_hbm, evid_hbm, *landed), (work, evid, *arrived)))]
    for load in loads:
        load.start()
    loads[0].wait()
    for lot, first, count in each(parts_out):
        loads[2 + lot].wait()
        for j in range(count):
            acc = work[first + j]
            for d in range(1, arrived[lot].shape[0]):
                acc = acc + arrived[lot][d, :, j * LANES:(j + 1) * LANES].astype(jnp.float32)
            work[first + j] = acc
    for c in range(CYCLES):
        for b in range(TURNS):
            at = (c * TURNS + b) * LANES
            for k in range(owned):
                j, row = spot(owned, c, b, k)
                sums_ref[k:k + 1, at:at + LANES] = work[j, row:row + 1, :]
    lane = lax.broadcasted_iota(jnp.int32, (1, LANES), 1)
    mass = jnp.zeros((1, LANES), jnp.float32)
    for k in range(owned):
        j, row = spot(owned, CYCLES, 0, k)
        tail = work[j, row:row + 1, :]
        mass = jnp.where(lane == k, tail + pltpu.roll(tail, LANES // 2, 1), mass)
    mass_ref[...] = mass[:, 0:owned]
    loads[1].wait()
    evid_ref[...] = evid[...]


def local(particles, references, inv_noise, assign):
    rows, width = particles.shape
    owned = references.shape[0]
    n = lax.axis_size("blk")
    chips = n // 2
    columns = -(-(CYCLES * TURNS + 1) * owned // DEPTH)
    parts_in = (columns - columns * 2 // 5, columns * 2 // 5)
    parts_out = (columns * 2 // 5, columns - columns * 2 // 5 - columns // 5, columns // 5)
    vmem = pl.BlockSpec(memory_space=pltpu.VMEM)
    hbm = pl.BlockSpec(memory_space=pltpu.HBM)

    def slots(count, parts):
        return [pltpu.VMEM((count, DEPTH, part * LANES), jnp.bfloat16) for part in parts]

    shares = pl.pallas_call(
        functools.partial(kernel, n, owned, parts_in, parts_out),
        out_shape=(
            *(jax.ShapeDtypeStruct((chips, DEPTH, part * LANES), jnp.bfloat16) for part in parts_out),
            jax.ShapeDtypeStruct((columns, DEPTH, LANES), jnp.float32),
            jax.ShapeDtypeStruct((1, rows), jnp.float32),
        ),
        in_specs=[hbm] * 4,
        out_specs=(hbm,) * (len(parts_out) + 2),
        scratch_shapes=[
            pltpu.VMEM((rows, width), jnp.bfloat16),
            pltpu.VMEM((width, rows), jnp.bfloat16),
            pltpu.VMEM((owned, width), jnp.bfloat16),
            pltpu.VMEM((1, rows), jnp.float32),
            pltpu.VMEM((TOPK, rows), jnp.int32),
            pltpu.VMEM((1, rows), jnp.float32),
            pltpu.VMEM((columns, n * DEPTH, LANES), jnp.float32),
            *slots(n, parts_in),
            *slots(chips, parts_out),
            *slots(chips, parts_out),
            *slots(chips, parts_out),
            pltpu.SemaphoreType.DMA,
            pltpu.SemaphoreType.DMA((3,)),
            pltpu.SemaphoreType.DMA((len(parts_out),)),
            pltpu.SemaphoreType.DMA,
            pltpu.SemaphoreType.DMA((len(parts_in), n)),
            pltpu.SemaphoreType.DMA((len(parts_in), n)),
            pltpu.SemaphoreType.DMA((len(parts_out),)),
            pltpu.SemaphoreType.DMA((len(parts_out),)),
            pltpu.SemaphoreType.DMA((len(parts_out), chips)),
            pltpu.SemaphoreType.DMA((len(parts_out), chips)),
        ],
        compiler_params=pltpu.CompilerParams(
            collective_id=0, has_side_effects=True, vmem_limit_bytes=64 * 1024 * 1024 - 65536),
        cost_estimate=pl.CostEstimate(
            flops=6 * rows * n * owned * ROT * width, bytes_accessed=2 * rows * width, transcendentals=rows * n * owned * ROT),
    )(particles, references, inv_noise.reshape(1, rows), assign.T)
    sums, mass, evid = pl.pallas_call(
        functools.partial(finish, owned, parts_out),
        out_shape=(
            jax.ShapeDtypeStruct((owned, width), jnp.float32),
            jax.ShapeDtypeStruct((1, owned), jnp.float32),
            jax.ShapeDtypeStruct((1, rows), jnp.float32),
        ),
        in_specs=[hbm] * (len(parts_out) + 2),
        out_specs=(vmem, vmem, vmem),
        scratch_shapes=[
            *slots(chips, parts_out),
            pltpu.VMEM((columns, DEPTH, LANES), jnp.float32),
            pltpu.VMEM((1, rows), jnp.float32),
            pltpu.SemaphoreType.DMA((len(parts_out) + 2,)),
        ],
        compiler_params=pltpu.CompilerParams(vmem_limit_bytes=64 * 1024 * 1024 - 65536),
    )(*shares)
    return sums, mass.reshape(owned), evid.reshape(rows)


def solution(mesh):
    placed = (
        P(("parts", "blk"), None),
        P(("parts", "blk"), None),
        P(("parts", "blk")),
        P(("parts", "blk"), None),
    )
    return jax.shard_map(
        local,
        mesh=mesh,
        in_specs=placed,
        out_specs=(P(("parts", "blk"), None), P(("parts", "blk")), P(("parts", "blk"))),
        check_vma=False,
    )
```

```python
import functools

import jax
import jax.numpy as jnp
from jax import lax
from jax.experimental import pallas as pl
from jax.experimental.pallas import tpu as pltpu
from jax.sharding import PartitionSpec as P

ROT = 12
TOPK = 2
CYCLES = 12
ANGLES = 384
STEP = ANGLES // ROT
LANES = 128
TURNS = ANGLES // LANES
SHIFTS = LANES // STEP
DEPTH = 16
MESH = pl.DeviceIdType.MESH


def spot(owned, c, b, k):
    at = (c * TURNS + b) * owned + k
    return at // DEPTH, at % DEPTH


def each(parts):
    first = 0
    for lot, count in enumerate(parts):
        yield lot, first, count
        first += count


def kernel(n, owned, parts_in, parts_out, x_hbm, refs_hbm, inv_hbm, assign_hbm, *scratch):
    lots = len(parts_in), len(parts_out)
    landed, scratch = scratch[:lots[1]], scratch[lots[1]:]
    own_hbm, evid_hbm, x_ref, xt_ref, refs_ref, inv_ref, assign_ref, evid_ref, work = scratch[:9]
    scratch = scratch[9:]
    held, scratch = scratch[:lots[0]], scratch[lots[0]:]
    swapped, scratch = scratch[:lots[1]], scratch[lots[1]:]
    part, scratch = scratch[:lots[1]], scratch[lots[1]:]
    x_sem, small_sem, own_sem, evid_sem, send1, recv1, swap_send, swap_recv, send2, recv2 = scratch
    me = lax.axis_index("blk")
    chips = n // 2
    chip, core = me // 2, lax.rem(me, 2)
    classes = n * owned
    rows = x_ref.shape[0]
    other = {"blk": chip * 2 + 1 - core}

    def ahead(d):
        return {"blk": lax.rem(chip + d, chips) * 2 + core}

    def behind(d):
        return {"blk": lax.rem(chip + chips - d, chips) * 2 + core}

    loads = [pltpu.make_async_copy(src, dst, small_sem.at[i]) for i, (src, dst) in enumerate(
        ((refs_hbm, refs_ref), (inv_hbm, inv_ref), (assign_hbm, assign_ref)))]
    loads.append(pltpu.make_async_copy(x_hbm, x_ref, x_sem))
    for load in loads:
        load.start()

    barrier = pltpu.get_barrier_semaphore()
    pl.semaphore_signal(barrier, inc=1, device_id=other, device_id_type=MESH)
    for d in range(1, chips):
        pl.semaphore_signal(barrier, inc=1, device_id=ahead(d), device_id_type=MESH)

    loads[0].wait()
    own = refs_ref[...].astype(jnp.float32)
    for j in range(work.shape[0]):
        work[j, 0:DEPTH, :] = jnp.zeros((DEPTH, LANES), jnp.float32)
    for c in range(CYCLES):
        for b in range(TURNS):
            at = (c * TURNS + b) * LANES
            for k in range(owned):
                j, row = spot(owned, c, b, k)
                work[j, row:row + 1, :] = own[k:k + 1, at:at + LANES]

    for lot, first, count in each(parts_in):
        for j in range(count):
            held[lot][0, :, j * LANES:(j + 1) * LANES] = work[first + j, 0:DEPTH, :].astype(jnp.bfloat16)

    pl.semaphore_wait(barrier, chips)

    def move(lot, src, dst, to):
        copy = pltpu.make_async_remote_copy(
            src_ref=held[lot].at[src], dst_ref=held[lot].at[dst], send_sem=send1.at[lot, dst],
            recv_sem=recv1.at[lot, dst], device_id=to, device_id_type=MESH)
        copy.start()
        return copy

    gathers = []
    for lot, _, _ in each(parts_in):
        copies = {d: move(lot, 0, d, ahead(d)) for d in range(1, chips)}
        copies[chips] = move(lot, 0, chips, other)
        gathers.append(copies)
    for load in loads[1:]:
        load.wait()

    def turn_over(start, stop):
        for at in range(start * LANES, min(stop * LANES, x_ref.shape[1]), LANES):
            xt_ref[at:at + LANES, :] = x_ref[:, at:at + LANES].T

    tiles = x_ref.shape[1] // LANES
    step = -(-tiles // (chips - 1))

    def shifted(c):
        blocks = [x_ref[:, (c * TURNS + b) * LANES:(c * TURNS + b + 1) * LANES] for b in range(TURNS)]
        return jnp.concatenate(
            [jnp.concatenate([blocks[(b + q) % TURNS] for b in range(TURNS)], axis=1)
             for q in range(TURNS)], axis=0)

    def forward(lot):
        copies = gathers[lot]
        for d in range(1, chips):
            if lot == 0:
                turn_over((d - 1) * step, d * step)
            copies[d].wait_recv()
            copies[chips + d] = move(lot, d, chips + d, other)

    def spread(lot, first, count):
        copies = gathers[lot]
        for d in range(chips):
            copies[chips + d].wait_recv()
        for d in range(n):
            for j in range(count):
                work[first + j, d * DEPTH:(d + 1) * DEPTH, :] = (
                    held[lot][d, :, j * LANES:(j + 1) * LANES].astype(jnp.float32))

    dots = jnp.zeros((ROT * classes, rows), jnp.float32)
    energy = jnp.zeros((classes, ANGLES), jnp.float32)
    turned = []
    lots_left = list(each(parts_in))
    ready = 0
    forward(0)
    for c in range(CYCLES):
        if c == 2:
            for lot in range(1, lots[0]):
                forward(lot)
        while ready <= spot(owned, c, TURNS - 1, owned - 1)[0]:
            lot, first, count = lots_left.pop(0)
            spread(lot, first, count)
            ready = first + count
        pieces = []
        for b in range(TURNS):
            column = []
            for k in range(owned):
                j, row = spot(owned, c, b, k)
                column.append(work[j, pl.ds(row, n, stride=DEPTH), :])
            pieces.append(jnp.concatenate(column, axis=0))
        ref_c = jnp.concatenate(pieces, axis=1)
        energy += ref_c * ref_c
        shifts = jnp.concatenate(
            [ref_c] + [pltpu.roll(ref_c, s * STEP, 1) for s in range(1, SHIFTS)], axis=0).astype(jnp.bfloat16)
        blocks = [shifts[:, b * LANES:(b + 1) * LANES] for b in range(TURNS)]
        turned.append(jnp.concatenate(
            [jnp.concatenate([blocks[(b - q) % TURNS] for b in range(TURNS)], axis=1)
             for q in range(TURNS)], axis=0))
        if len(turned) == 2:
            dots += jnp.dot(
                jnp.concatenate(turned, axis=1), xt_ref[(c - 1) * ANGLES:(c + 1) * ANGLES, :],
                preferred_element_type=jnp.float32)
            turned = []

    half = 0.5 * jnp.sum(energy, axis=1, keepdims=True)
    logits = inv_ref[...] * (dots - jnp.concatenate([half] * ROT, axis=0))
    top = jnp.max(logits, axis=0, keepdims=True)
    scaled = jnp.exp(logits - top)
    total = jnp.sum(scaled, axis=0, keepdims=True)
    evid_ref[...] = top + jnp.log(total)
    evid_copy = pltpu.make_async_copy(evid_ref, evid_hbm, evid_sem)
    evid_copy.start()

    slot = lax.broadcasted_iota(jnp.int32, (n, rows), 0)
    side = (slot >= chips).astype(jnp.int32)
    source = chip - (slot - side * chips)
    source = jnp.where(source < 0, source + chips, source) * 2 + jnp.where(side == 0, core, 1 - core)
    names = jnp.concatenate([source * owned + k for k in range(owned)], axis=0)
    named = names == assign_ref[0:1, :]
    for j in range(1, TOPK):
        named = jnp.logical_or(named, names == assign_ref[j:j + 1, :])
    picked = jnp.where(named, 1.0 / total, 0.0)
    weight = scaled * jnp.concatenate([picked] * ROT, axis=0)
    mass = functools.reduce(jnp.add, [weight[r * classes:(r + 1) * classes] for r in range(ROT)])
    mass = jnp.sum(mass, axis=1, keepdims=True)
    turn = SHIFTS * classes
    weight = jnp.concatenate([weight[q * turn:(q + 1) * turn] for q in range(TURNS)], axis=1)
    high = weight.astype(jnp.bfloat16)

    def put(c, b, value):
        for k in range(owned):
            j, row = spot(owned, c, b, k)
            work[j, pl.ds(row, n, stride=DEPTH), :] = value[k * n:(k + 1) * n]

    mass = jnp.broadcast_to(mass, (classes, LANES))
    mass_high = mass.astype(jnp.bfloat16).astype(jnp.float32)
    lane = lax.broadcasted_iota(jnp.int32, (classes, LANES), 1)
    put(CYCLES, 0, jnp.where(lane < LANES // 2, mass_high, mass - mass_high))

    swaps, scatters, own_copies = [], [], []

    def give(lot, first, count):
        copy = pltpu.make_async_remote_copy(
            src_ref=work.at[first:first + count, chips * DEPTH:n * DEPTH], dst_ref=swapped[lot],
            send_sem=swap_send.at[lot], recv_sem=swap_recv.at[lot], device_id=other, device_id_type=MESH)
        copy.start()
        swaps.append(copy)

    def pass_on(lot, first, count):
        swaps[lot].wait_recv()
        for d in (*range(1, chips), 0):
            for j in range(count):
                both_cores = (work[first + j, d * DEPTH:(d + 1) * DEPTH, :]
                              + swapped[lot][j, d * DEPTH:(d + 1) * DEPTH, :])
                if d:
                    part[lot][d, :, j * LANES:(j + 1) * LANES] = both_cores.astype(jnp.bfloat16)
                else:
                    work[first + j, 0:DEPTH, :] = both_cores
            if d:
                copy = pltpu.make_async_remote_copy(
                    src_ref=part[lot].at[d], dst_ref=landed[lot].at[d], send_sem=send2.at[lot, d],
                    recv_sem=recv2.at[lot, d], device_id=behind(d), device_id_type=MESH)
                copy.start()
                scatters.append(copy)
        copy = pltpu.make_async_copy(
            work.at[first:first + count, 0:DEPTH], own_hbm.at[first:first + count], own_sem.at[lot])
        copy.start()
        own_copies.append(copy)

    lots_left = list(each(parts_out))
    given = []
    for c in range(CYCLES):
        if c % 2 == 0:
            mixed = jnp.dot(
                high, jnp.concatenate([shifted(c), shifted(c + 1)], axis=1), preferred_element_type=jnp.float32)
        at = c % 2 * ANGLES
        out = None
        for s in range(SHIFTS):
            piece = mixed[s * classes:(s + 1) * classes, at:at + ANGLES]
            if s:
                piece = pltpu.roll(piece, ANGLES - s * STEP, 1)
            out = piece if out is None else out + piece
        for b in range(TURNS):
            put(c, b, out[:, b * LANES:(b + 1) * LANES])
        if given and given[0][0] + 3 <= c:
            pass_on(*given.pop(0)[1])
        done = (c + 1) * TURNS * owned
        while lots_left and (done >= (lots_left[0][1] + lots_left[0][2]) * DEPTH or c == CYCLES - 1):
            give(*lots_left[0])
            given.append((c, lots_left.pop(0)))
    for _, lot in given:
        pass_on(*lot)

    for copies in gathers:
        for copy in copies.values():
            copy.wait_send()
    for copy in swaps:
        copy.wait_send()
    for copy in own_copies:
        copy.wait()
    evid_copy.wait()
    for copy in scatters:
        copy.wait()


def finish(owned, parts_out, *refs):
    lots = len(parts_out)
    landed, (own_hbm, evid_hbm, sums_ref, mass_ref, evid_ref) = refs[:lots], refs[lots:lots + 5]
    arrived, (work, evid, sems) = refs[lots + 5:-3], refs[-3:]
    loads = [pltpu.make_async_copy(src, dst, sems.at[i]) for i, (src, dst) in enumerate(
        zip((own_hbm, evid_hbm, *landed), (work, evid, *arrived)))]
    for load in loads:
        load.start()
    loads[0].wait()
    for lot, first, count in each(parts_out):
        loads[2 + lot].wait()
        for j in range(count):
            acc = work[first + j]
            for d in range(1, arrived[lot].shape[0]):
                acc = acc + arrived[lot][d, :, j * LANES:(j + 1) * LANES].astype(jnp.float32)
            work[first + j] = acc
    for c in range(CYCLES):
        for b in range(TURNS):
            at = (c * TURNS + b) * LANES
            for k in range(owned):
                j, row = spot(owned, c, b, k)
                sums_ref[k:k + 1, at:at + LANES] = work[j, row:row + 1, :]
    lane = lax.broadcasted_iota(jnp.int32, (1, LANES), 1)
    mass = jnp.zeros((1, LANES), jnp.float32)
    for k in range(owned):
        j, row = spot(owned, CYCLES, 0, k)
        tail = work[j, row:row + 1, :]
        mass = jnp.where(lane == k, tail + pltpu.roll(tail, LANES // 2, 1), mass)
    mass_ref[...] = mass[:, 0:owned]
    loads[1].wait()
    evid_ref[...] = evid[...]


def local(particles, references, inv_noise, assign):
    rows, width = particles.shape
    owned = references.shape[0]
    n = lax.axis_size("blk")
    chips = n // 2
    columns = -(-(CYCLES * TURNS + 1) * owned // DEPTH)
    parts_in = (columns - columns * 2 // 5, columns * 2 // 5)
    parts_out = (columns * 2 // 5, columns - columns * 2 // 5 - columns // 5, columns // 5)
    vmem = pl.BlockSpec(memory_space=pltpu.VMEM)
    hbm = pl.BlockSpec(memory_space=pltpu.HBM)

    def slots(count, parts):
        return [pltpu.VMEM((count, DEPTH, part * LANES), jnp.bfloat16) for part in parts]

    shares = pl.pallas_call(
        functools.partial(kernel, n, owned, parts_in, parts_out),
        out_shape=(
            *(jax.ShapeDtypeStruct((chips, DEPTH, part * LANES), jnp.bfloat16) for part in parts_out),
            jax.ShapeDtypeStruct((columns, DEPTH, LANES), jnp.float32),
            jax.ShapeDtypeStruct((1, rows), jnp.float32),
        ),
        in_specs=[hbm] * 4,
        out_specs=(hbm,) * (len(parts_out) + 2),
        scratch_shapes=[
            pltpu.VMEM((rows, width), jnp.bfloat16),
            pltpu.VMEM((width, rows), jnp.bfloat16),
            pltpu.VMEM((owned, width), jnp.bfloat16),
            pltpu.VMEM((1, rows), jnp.float32),
            pltpu.VMEM((TOPK, rows), jnp.int32),
            pltpu.VMEM((1, rows), jnp.float32),
            pltpu.VMEM((columns, n * DEPTH, LANES), jnp.float32),
            *slots(n, parts_in),
            *(pltpu.VMEM((part, chips * DEPTH, LANES), jnp.float32) for part in parts_out),
            *slots(chips, parts_out),
            pltpu.SemaphoreType.DMA,
            pltpu.SemaphoreType.DMA((3,)),
            pltpu.SemaphoreType.DMA((len(parts_out),)),
            pltpu.SemaphoreType.DMA,
            pltpu.SemaphoreType.DMA((len(parts_in), n)),
            pltpu.SemaphoreType.DMA((len(parts_in), n)),
            pltpu.SemaphoreType.DMA((len(parts_out),)),
            pltpu.SemaphoreType.DMA((len(parts_out),)),
            pltpu.SemaphoreType.DMA((len(parts_out), chips)),
            pltpu.SemaphoreType.DMA((len(parts_out), chips)),
        ],
        compiler_params=pltpu.CompilerParams(
            collective_id=0, has_side_effects=True, vmem_limit_bytes=64 * 1024 * 1024 - 65536),
        cost_estimate=pl.CostEstimate(
            flops=6 * rows * n * owned * ROT * width, bytes_accessed=2 * rows * width, transcendentals=rows * n * owned * ROT),
    )(particles, references, inv_noise.reshape(1, rows), assign.T)
    sums, mass, evid = pl.pallas_call(
        functools.partial(finish, owned, parts_out),
        out_shape=(
            jax.ShapeDtypeStruct((owned, width), jnp.float32),
            jax.ShapeDtypeStruct((1, owned), jnp.float32),
            jax.ShapeDtypeStruct((1, rows), jnp.float32),
        ),
        in_specs=[hbm] * (len(parts_out) + 2),
        out_specs=(vmem, vmem, vmem),
        scratch_shapes=[
            *slots(chips, parts_out),
            pltpu.VMEM((columns, DEPTH, LANES), jnp.float32),
            pltpu.VMEM((1, rows), jnp.float32),
            pltpu.SemaphoreType.DMA((len(parts_out) + 2,)),
        ],
        compiler_params=pltpu.CompilerParams(vmem_limit_bytes=64 * 1024 * 1024 - 65536),
    )(*shares)
    return sums, mass.reshape(owned), evid.reshape(rows)


def solution(mesh):
    placed = (
        P(("parts", "blk"), None),
        P(("parts", "blk"), None),
        P(("parts", "blk")),
        P(("parts", "blk"), None),
    )
    return jax.shard_map(
        local,
        mesh=mesh,
        in_specs=placed,
        out_specs=(P(("parts", "blk"), None), P(("parts", "blk")), P(("parts", "blk"))),
        check_vma=False,
    )
```

```python
import functools

import jax
import jax.numpy as jnp
from jax import lax
from jax.experimental import pallas as pl
from jax.experimental.pallas import tpu as pltpu
from jax.sharding import PartitionSpec as P

ROT = 12
TOPK = 2
CYCLES = 12
ANGLES = 384
STEP = ANGLES // ROT
LANES = 128
TURNS = ANGLES // LANES
SHIFTS = LANES // STEP
DEPTH = 16
MESH = pl.DeviceIdType.MESH


def spot(owned, c, b, k):
    at = (c * TURNS + b) * owned + k
    return at // DEPTH, at % DEPTH


def each(parts):
    first = 0
    for lot, count in enumerate(parts):
        yield lot, first, count
        first += count


def kernel(n, owned, parts_in, parts_out, x_hbm, refs_hbm, inv_hbm, assign_hbm, *scratch):
    lots = len(parts_in), len(parts_out)
    landed, scratch = scratch[:lots[1]], scratch[lots[1]:]
    own_hbm, evid_hbm, x_ref, xt_ref, refs_ref, inv_ref, assign_ref, evid_ref, work = scratch[:9]
    scratch = scratch[9:]
    held, scratch = scratch[:lots[0]], scratch[lots[0]:]
    swapped, scratch = scratch[:lots[1]], scratch[lots[1]:]
    part, scratch = scratch[:lots[1]], scratch[lots[1]:]
    x_sem, small_sem, own_sem, evid_sem, send1, recv1, swap_send, swap_recv, send2, recv2 = scratch
    me = lax.axis_index("blk")
    chips = n // 2
    chip, core = me // 2, lax.rem(me, 2)
    classes = n * owned
    rows = x_ref.shape[0]
    other = {"blk": chip * 2 + 1 - core}

    def ahead(d):
        return {"blk": lax.rem(chip + d, chips) * 2 + core}

    def behind(d):
        return {"blk": lax.rem(chip + chips - d, chips) * 2 + core}

    loads = [pltpu.make_async_copy(src, dst, small_sem.at[i]) for i, (src, dst) in enumerate(
        ((refs_hbm, refs_ref), (inv_hbm, inv_ref), (assign_hbm, assign_ref)))]
    loads.append(pltpu.make_async_copy(x_hbm, x_ref, x_sem))
    for load in loads:
        load.start()

    barrier = pltpu.get_barrier_semaphore()
    pl.semaphore_signal(barrier, inc=1, device_id=other, device_id_type=MESH)
    for d in range(1, chips):
        pl.semaphore_signal(barrier, inc=1, device_id=ahead(d), device_id_type=MESH)

    loads[0].wait()
    own = refs_ref[...].astype(jnp.float32)
    for j in range(work.shape[0]):
        work[j, 0:DEPTH, :] = jnp.zeros((DEPTH, LANES), jnp.float32)
    for c in range(CYCLES):
        for b in range(TURNS):
            at = (c * TURNS + b) * LANES
            for k in range(owned):
                j, row = spot(owned, c, b, k)
                work[j, row:row + 1, :] = own[k:k + 1, at:at + LANES]

    for lot, first, count in each(parts_in):
        for j in range(count):
            held[lot][0, :, j * LANES:(j + 1) * LANES] = work[first + j, 0:DEPTH, :].astype(jnp.bfloat16)

    pl.semaphore_wait(barrier, chips)

    def move(lot, src, dst, to):
        copy = pltpu.make_async_remote_copy(
            src_ref=held[lot].at[src], dst_ref=held[lot].at[dst], send_sem=send1.at[lot, dst],
            recv_sem=recv1.at[lot, dst], device_id=to, device_id_type=MESH)
        copy.start()
        return copy

    gathers = []
    for lot, _, _ in each(parts_in):
        copies = {d: move(lot, 0, d, ahead(d)) for d in range(1, chips)}
        copies[chips] = move(lot, 0, chips, other)
        gathers.append(copies)
    for load in loads[1:]:
        load.wait()

    def turn_over(start, stop):
        for at in range(start * LANES, min(stop * LANES, x_ref.shape[1]), LANES):
            xt_ref[at:at + LANES, :] = x_ref[:, at:at + LANES].T

    tiles = x_ref.shape[1] // LANES
    step = -(-tiles // (chips - 1))

    def shifted(c):
        blocks = [x_ref[:, (c * TURNS + b) * LANES:(c * TURNS + b + 1) * LANES] for b in range(TURNS)]
        return jnp.concatenate(
            [jnp.concatenate([blocks[(b + q) % TURNS] for b in range(TURNS)], axis=1)
             for q in range(TURNS)], axis=0)

    def forward(lot):
        copies = gathers[lot]
        for d in range(1, chips):
            if lot == 0:
                turn_over((d - 1) * step, d * step)
            copies[d].wait_recv()
            copies[chips + d] = move(lot, d, chips + d, other)

    def spread(lot, first, count):
        copies = gathers[lot]
        for d in range(chips):
            copies[chips + d].wait_recv()
        for d in range(n):
            for j in range(count):
                work[first + j, d * DEPTH:(d + 1) * DEPTH, :] = (
                    held[lot][d, :, j * LANES:(j + 1) * LANES].astype(jnp.float32))

    dots = jnp.zeros((ROT * classes, rows), jnp.float32)
    energy = jnp.zeros((classes, ANGLES), jnp.float32)
    turned = []
    lots_left = list(each(parts_in))
    ready = 0
    forward(0)
    for c in range(CYCLES):
        if c == 2:
            for lot in range(1, lots[0]):
                forward(lot)
        while ready <= spot(owned, c, TURNS - 1, owned - 1)[0]:
            lot, first, count = lots_left.pop(0)
            spread(lot, first, count)
            ready = first + count
        pieces = []
        for b in range(TURNS):
            column = []
            for k in range(owned):
                j, row = spot(owned, c, b, k)
                column.append(work[j, pl.ds(row, n, stride=DEPTH), :])
            pieces.append(jnp.concatenate(column, axis=0))
        ref_c = jnp.concatenate(pieces, axis=1)
        energy += ref_c * ref_c
        shifts = jnp.concatenate(
            [ref_c] + [pltpu.roll(ref_c, s * STEP, 1) for s in range(1, SHIFTS)], axis=0).astype(jnp.bfloat16)
        blocks = [shifts[:, b * LANES:(b + 1) * LANES] for b in range(TURNS)]
        turned.append(jnp.concatenate(
            [jnp.concatenate([blocks[(b - q) % TURNS] for b in range(TURNS)], axis=1)
             for q in range(TURNS)], axis=0))
        if len(turned) == 2:
            dots += jnp.dot(
                jnp.concatenate(turned, axis=1), xt_ref[(c - 1) * ANGLES:(c + 1) * ANGLES, :],
                preferred_element_type=jnp.float32)
            turned = []

    half = 0.5 * jnp.sum(energy, axis=1, keepdims=True)
    logits = inv_ref[...] * (dots - jnp.concatenate([half] * ROT, axis=0))
    top = jnp.max(logits, axis=0, keepdims=True)
    scaled = jnp.exp(logits - top)
    total = jnp.sum(scaled, axis=0, keepdims=True)
    evid_ref[...] = top + jnp.log(total)
    evid_copy = pltpu.make_async_copy(evid_ref, evid_hbm, evid_sem)
    evid_copy.start()

    slot = lax.broadcasted_iota(jnp.int32, (n, rows), 0)
    side = (slot >= chips).astype(jnp.int32)
    source = chip - (slot - side * chips)
    source = jnp.where(source < 0, source + chips, source) * 2 + jnp.where(side == 0, core, 1 - core)
    names = jnp.concatenate([source * owned + k for k in range(owned)], axis=0)
    named = names == assign_ref[0:1, :]
    for j in range(1, TOPK):
        named = jnp.logical_or(named, names == assign_ref[j:j + 1, :])
    picked = jnp.where(named, 1.0 / total, 0.0)
    weight = scaled * jnp.concatenate([picked] * ROT, axis=0)
    mass = functools.reduce(jnp.add, [weight[r * classes:(r + 1) * classes] for r in range(ROT)])
    mass = jnp.sum(mass, axis=1, keepdims=True)
    turn = SHIFTS * classes
    weight = jnp.concatenate([weight[q * turn:(q + 1) * turn] for q in range(TURNS)], axis=1)
    high = weight.astype(jnp.bfloat16)

    def put(c, b, value):
        for k in range(owned):
            j, row = spot(owned, c, b, k)
            work[j, pl.ds(row, n, stride=DEPTH), :] = value[k * n:(k + 1) * n]

    mass = jnp.broadcast_to(mass, (classes, LANES))
    mass_high = mass.astype(jnp.bfloat16).astype(jnp.float32)
    lane = lax.broadcasted_iota(jnp.int32, (classes, LANES), 1)
    put(CYCLES, 0, jnp.where(lane < LANES // 2, mass_high, mass - mass_high))

    swaps, scatters, own_copies = [], [], []

    def give(lot, first, count):
        copy = pltpu.make_async_remote_copy(
            src_ref=work.at[first:first + count, chips * DEPTH:n * DEPTH], dst_ref=swapped[lot],
            send_sem=swap_send.at[lot], recv_sem=swap_recv.at[lot], device_id=other, device_id_type=MESH)
        copy.start()
        swaps.append(copy)

    def pass_on(lot, first, count):
        swaps[lot].wait_recv()
        for d in (*range(1, chips), 0):
            for j in range(count):
                both_cores = (work[first + j, d * DEPTH:(d + 1) * DEPTH, :]
                              + swapped[lot][j, d * DEPTH:(d + 1) * DEPTH, :])
                if d:
                    part[lot][d, :, j * LANES:(j + 1) * LANES] = both_cores.astype(jnp.bfloat16)
                else:
                    work[first + j, 0:DEPTH, :] = both_cores
            if d:
                copy = pltpu.make_async_remote_copy(
                    src_ref=part[lot].at[d], dst_ref=landed[lot].at[d], send_sem=send2.at[lot, d],
                    recv_sem=recv2.at[lot, d], device_id=behind(d), device_id_type=MESH)
                copy.start()
                scatters.append(copy)
        copy = pltpu.make_async_copy(
            work.at[first:first + count, 0:DEPTH], own_hbm.at[first:first + count], own_sem.at[lot])
        copy.start()
        own_copies.append(copy)

    lots_left = list(each(parts_out))
    given = []
    for c in range(CYCLES):
        if c % 2 == 0:
            mixed = jnp.dot(
                high, jnp.concatenate([shifted(c), shifted(c + 1)], axis=1), preferred_element_type=jnp.float32)
        at = c % 2 * ANGLES
        out = None
        for s in range(SHIFTS):
            piece = mixed[s * classes:(s + 1) * classes, at:at + ANGLES]
            if s:
                piece = pltpu.roll(piece, ANGLES - s * STEP, 1)
            out = piece if out is None else out + piece
        for b in range(TURNS):
            put(c, b, out[:, b * LANES:(b + 1) * LANES])
        if given and given[0][0] + 3 <= c:
            pass_on(*given.pop(0)[1])
        done = (c + 1) * TURNS * owned
        while lots_left and (done >= (lots_left[0][1] + lots_left[0][2]) * DEPTH or c == CYCLES - 1):
            give(*lots_left[0])
            given.append((c, lots_left.pop(0)))
    for _, lot in given:
        pass_on(*lot)

    for copies in gathers:
        for copy in copies.values():
            copy.wait_send()
    for copy in swaps:
        copy.wait_send()
    for copy in own_copies:
        copy.wait()
    evid_copy.wait()
    for copy in scatters:
        copy.wait()


def finish(owned, parts_out, *refs):
    lots = len(parts_out)
    landed, (own_hbm, evid_hbm, sums_ref, mass_ref, evid_ref) = refs[:lots], refs[lots:lots + 5]
    arrived, (work, evid, sems) = refs[lots + 5:-3], refs[-3:]
    loads = [pltpu.make_async_copy(src, dst, sems.at[i]) for i, (src, dst) in enumerate(
        zip((own_hbm, evid_hbm, *landed), (work, evid, *arrived)))]
    for load in loads:
        load.start()
    loads[0].wait()
    for lot, first, count in each(parts_out):
        loads[2 + lot].wait()
        for j in range(count):
            acc = work[first + j]
            for d in range(1, arrived[lot].shape[0]):
                acc = acc + arrived[lot][d, :, j * LANES:(j + 1) * LANES].astype(jnp.float32)
            work[first + j] = acc
    for c in range(CYCLES):
        for b in range(TURNS):
            at = (c * TURNS + b) * LANES
            for k in range(owned):
                j, row = spot(owned, c, b, k)
                sums_ref[k:k + 1, at:at + LANES] = work[j, row:row + 1, :]
    lane = lax.broadcasted_iota(jnp.int32, (1, LANES), 1)
    mass = jnp.zeros((1, LANES), jnp.float32)
    for k in range(owned):
        j, row = spot(owned, CYCLES, 0, k)
        tail = work[j, row:row + 1, :]
        mass = jnp.where(lane == k, tail + pltpu.roll(tail, LANES // 2, 1), mass)
    mass_ref[...] = mass[:, 0:owned]
    loads[1].wait()
    evid_ref[...] = evid[...]


def local(particles, references, inv_noise, assign):
    rows, width = particles.shape
    owned = references.shape[0]
    n = lax.axis_size("blk")
    chips = n // 2
    columns = -(-(CYCLES * TURNS + 1) * owned // DEPTH)
    parts_in = (columns - columns * 2 // 5, columns * 2 // 5)
    parts_out = (columns * 2 // 5, columns // 5, columns - columns * 2 // 5 - columns // 5)
    vmem = pl.BlockSpec(memory_space=pltpu.VMEM)
    hbm = pl.BlockSpec(memory_space=pltpu.HBM)

    def slots(count, parts):
        return [pltpu.VMEM((count, DEPTH, part * LANES), jnp.bfloat16) for part in parts]

    shares = pl.pallas_call(
        functools.partial(kernel, n, owned, parts_in, parts_out),
        out_shape=(
            *(jax.ShapeDtypeStruct((chips, DEPTH, part * LANES), jnp.bfloat16) for part in parts_out),
            jax.ShapeDtypeStruct((columns, DEPTH, LANES), jnp.float32),
            jax.ShapeDtypeStruct((1, rows), jnp.float32),
        ),
        in_specs=[hbm] * 4,
        out_specs=(hbm,) * (len(parts_out) + 2),
        scratch_shapes=[
            pltpu.VMEM((rows, width), jnp.bfloat16),
            pltpu.VMEM((width, rows), jnp.bfloat16),
            pltpu.VMEM((owned, width), jnp.bfloat16),
            pltpu.VMEM((1, rows), jnp.float32),
            pltpu.VMEM((TOPK, rows), jnp.int32),
            pltpu.VMEM((1, rows), jnp.float32),
            pltpu.VMEM((columns, n * DEPTH, LANES), jnp.float32),
            *slots(n, parts_in),
            *(pltpu.VMEM((part, chips * DEPTH, LANES), jnp.float32) for part in parts_out),
            *slots(chips, parts_out),
            pltpu.SemaphoreType.DMA,
            pltpu.SemaphoreType.DMA((3,)),
            pltpu.SemaphoreType.DMA((len(parts_out),)),
            pltpu.SemaphoreType.DMA,
            pltpu.SemaphoreType.DMA((len(parts_in), n)),
            pltpu.SemaphoreType.DMA((len(parts_in), n)),
            pltpu.SemaphoreType.DMA((len(parts_out),)),
            pltpu.SemaphoreType.DMA((len(parts_out),)),
            pltpu.SemaphoreType.DMA((len(parts_out), chips)),
            pltpu.SemaphoreType.DMA((len(parts_out), chips)),
        ],
        compiler_params=pltpu.CompilerParams(
            collective_id=0, has_side_effects=True, vmem_limit_bytes=64 * 1024 * 1024 - 65536),
        cost_estimate=pl.CostEstimate(
            flops=6 * rows * n * owned * ROT * width, bytes_accessed=2 * rows * width, transcendentals=rows * n * owned * ROT),
    )(particles, references, inv_noise.reshape(1, rows), assign.T)
    sums, mass, evid = pl.pallas_call(
        functools.partial(finish, owned, parts_out),
        out_shape=(
            jax.ShapeDtypeStruct((owned, width), jnp.float32),
            jax.ShapeDtypeStruct((1, owned), jnp.float32),
            jax.ShapeDtypeStruct((1, rows), jnp.float32),
        ),
        in_specs=[hbm] * (len(parts_out) + 2),
        out_specs=(vmem, vmem, vmem),
        scratch_shapes=[
            *slots(chips, parts_out),
            pltpu.VMEM((columns, DEPTH, LANES), jnp.float32),
            pltpu.VMEM((1, rows), jnp.float32),
            pltpu.SemaphoreType.DMA((len(parts_out) + 2,)),
        ],
        compiler_params=pltpu.CompilerParams(vmem_limit_bytes=64 * 1024 * 1024 - 65536),
    )(*shares)
    return sums, mass.reshape(owned), evid.reshape(rows)


def solution(mesh):
    placed = (
        P(("parts", "blk"), None),
        P(("parts", "blk"), None),
        P(("parts", "blk")),
        P(("parts", "blk"), None),
    )
    return jax.shard_map(
        local,
        mesh=mesh,
        in_specs=placed,
        out_specs=(P(("parts", "blk"), None), P(("parts", "blk")), P(("parts", "blk"))),
        check_vma=False,
    )
```

```python
import functools

import jax
import jax.numpy as jnp
from jax import lax
from jax.experimental import pallas as pl
from jax.experimental.pallas import tpu as pltpu
from jax.sharding import PartitionSpec as P

ROT = 12
TOPK = 2
CYCLES = 12
ANGLES = 384
STEP = ANGLES // ROT
LANES = 128
TURNS = ANGLES // LANES
SHIFTS = LANES // STEP
DEPTH = 16
MESH = pl.DeviceIdType.MESH


def spot(owned, c, b, k):
    at = (c * TURNS + b) * owned + k
    return at // DEPTH, at % DEPTH


def each(parts):
    first = 0
    for lot, count in enumerate(parts):
        yield lot, first, count
        first += count


def kernel(n, owned, parts_in, parts_out, x_hbm, refs_hbm, inv_hbm, assign_hbm, *scratch):
    lots = len(parts_in), len(parts_out)
    landed, scratch = scratch[:lots[1]], scratch[lots[1]:]
    own_hbm, evid_hbm, x_ref, xt_ref, refs_ref, inv_ref, assign_ref, evid_ref, work = scratch[:9]
    scratch = scratch[9:]
    held, scratch = scratch[:lots[0]], scratch[lots[0]:]
    swapped, scratch = scratch[:lots[1]], scratch[lots[1]:]
    part, scratch = scratch[:lots[1]], scratch[lots[1]:]
    x_sem, small_sem, own_sem, evid_sem, send1, recv1, swap_send, swap_recv, send2, recv2 = scratch
    me = lax.axis_index("blk")
    chips = n // 2
    chip, core = me // 2, lax.rem(me, 2)
    classes = n * owned
    rows = x_ref.shape[0]
    other = {"blk": chip * 2 + 1 - core}

    def ahead(d):
        return {"blk": lax.rem(chip + d, chips) * 2 + core}

    def behind(d):
        return {"blk": lax.rem(chip + chips - d, chips) * 2 + core}

    loads = [pltpu.make_async_copy(src, dst, small_sem.at[i]) for i, (src, dst) in enumerate(
        ((refs_hbm, refs_ref), (inv_hbm, inv_ref), (assign_hbm, assign_ref)))]
    loads.append(pltpu.make_async_copy(x_hbm, x_ref, x_sem))
    for load in loads:
        load.start()

    barrier = pltpu.get_barrier_semaphore()
    pl.semaphore_signal(barrier, inc=1, device_id=other, device_id_type=MESH)
    for d in range(1, chips):
        pl.semaphore_signal(barrier, inc=1, device_id=ahead(d), device_id_type=MESH)

    loads[0].wait()
    own = refs_ref[...].astype(jnp.float32)
    for j in range(work.shape[0]):
        work[j, 0:DEPTH, :] = jnp.zeros((DEPTH, LANES), jnp.float32)
    for c in range(CYCLES):
        for b in range(TURNS):
            at = (c * TURNS + b) * LANES
            for k in range(owned):
                j, row = spot(owned, c, b, k)
                work[j, row:row + 1, :] = own[k:k + 1, at:at + LANES]

    for lot, first, count in each(parts_in):
        for j in range(count):
            held[lot][0, :, j * LANES:(j + 1) * LANES] = work[first + j, 0:DEPTH, :].astype(jnp.bfloat16)

    pl.semaphore_wait(barrier, chips)

    def move(lot, src, dst, to):
        copy = pltpu.make_async_remote_copy(
            src_ref=held[lot].at[src], dst_ref=held[lot].at[dst], send_sem=send1.at[lot, dst],
            recv_sem=recv1.at[lot, dst], device_id=to, device_id_type=MESH)
        copy.start()
        return copy

    gathers = []
    for lot, _, _ in each(parts_in):
        copies = {d: move(lot, 0, d, ahead(d)) for d in range(1, chips)}
        copies[chips] = move(lot, 0, chips, other)
        gathers.append(copies)
    for load in loads[1:]:
        load.wait()

    def turn_over(start, stop):
        for at in range(start * LANES, min(stop * LANES, x_ref.shape[1]), LANES):
            xt_ref[at:at + LANES, :] = x_ref[:, at:at + LANES].T

    tiles = x_ref.shape[1] // LANES
    step = -(-tiles // (chips - 1))

    def shifted(c):
        blocks = [x_ref[:, (c * TURNS + b) * LANES:(c * TURNS + b + 1) * LANES] for b in range(TURNS)]
        return jnp.concatenate(
            [jnp.concatenate([blocks[(b + q) % TURNS] for b in range(TURNS)], axis=1)
             for q in range(TURNS)], axis=0)

    def forward(lot):
        copies = gathers[lot]
        for d in range(1, chips):
            if lot == 0:
                turn_over((d - 1) * step, d * step)
            copies[d].wait_recv()
            copies[chips + d] = move(lot, d, chips + d, other)

    def spread(lot, first, count):
        copies = gathers[lot]
        for d in range(chips):
            copies[chips + d].wait_recv()
        for d in range(n):
            for j in range(count):
                work[first + j, d * DEPTH:(d + 1) * DEPTH, :] = (
                    held[lot][d, :, j * LANES:(j + 1) * LANES].astype(jnp.float32))

    dots = jnp.zeros((ROT * classes, rows), jnp.float32)
    energy = jnp.zeros((classes, ANGLES), jnp.float32)
    turned = []
    lots_left = list(each(parts_in))
    ready = 0
    forward(0)
    for c in range(CYCLES):
        if c == 2:
            for lot in range(1, lots[0]):
                forward(lot)
        while ready <= spot(owned, c, TURNS - 1, owned - 1)[0]:
            lot, first, count = lots_left.pop(0)
            spread(lot, first, count)
            ready = first + count
        pieces = []
        for b in range(TURNS):
            column = []
            for k in range(owned):
                j, row = spot(owned, c, b, k)
                column.append(work[j, pl.ds(row, n, stride=DEPTH), :])
            pieces.append(jnp.concatenate(column, axis=0))
        ref_c = jnp.concatenate(pieces, axis=1)
        energy += ref_c * ref_c
        shifts = jnp.concatenate(
            [ref_c] + [pltpu.roll(ref_c, s * STEP, 1) for s in range(1, SHIFTS)], axis=0).astype(jnp.bfloat16)
        blocks = [shifts[:, b * LANES:(b + 1) * LANES] for b in range(TURNS)]
        turned.append(jnp.concatenate(
            [jnp.concatenate([blocks[(b - q) % TURNS] for b in range(TURNS)], axis=1)
             for q in range(TURNS)], axis=0))
        if len(turned) == 2:
            dots += jnp.dot(
                jnp.concatenate(turned, axis=1), xt_ref[(c - 1) * ANGLES:(c + 1) * ANGLES, :],
                preferred_element_type=jnp.float32)
            turned = []

    half = 0.5 * jnp.sum(energy, axis=1, keepdims=True)
    logits = inv_ref[...] * (dots - jnp.concatenate([half] * ROT, axis=0))
    top = jnp.max(logits, axis=0, keepdims=True)
    scaled = jnp.exp(logits - top)
    total = jnp.sum(scaled, axis=0, keepdims=True)
    evid_ref[...] = top + jnp.log(total)
    evid_copy = pltpu.make_async_copy(evid_ref, evid_hbm, evid_sem)
    evid_copy.start()

    slot = lax.broadcasted_iota(jnp.int32, (n, rows), 0)
    side = (slot >= chips).astype(jnp.int32)
    source = chip - (slot - side * chips)
    source = jnp.where(source < 0, source + chips, source) * 2 + jnp.where(side == 0, core, 1 - core)
    names = jnp.concatenate([source * owned + k for k in range(owned)], axis=0)
    named = names == assign_ref[0:1, :]
    for j in range(1, TOPK):
        named = jnp.logical_or(named, names == assign_ref[j:j + 1, :])
    picked = jnp.where(named, 1.0 / total, 0.0)
    weight = scaled * jnp.concatenate([picked] * ROT, axis=0)
    mass = functools.reduce(jnp.add, [weight[r * classes:(r + 1) * classes] for r in range(ROT)])
    mass = jnp.sum(mass, axis=1, keepdims=True)
    turn = SHIFTS * classes
    weight = jnp.concatenate([weight[q * turn:(q + 1) * turn] for q in range(TURNS)], axis=1)
    high = weight.astype(jnp.bfloat16)

    def put(c, b, value):
        for k in range(owned):
            j, row = spot(owned, c, b, k)
            work[j, pl.ds(row, n, stride=DEPTH), :] = value[k * n:(k + 1) * n]

    mass = jnp.broadcast_to(mass, (classes, LANES))
    mass_high = mass.astype(jnp.bfloat16).astype(jnp.float32)
    lane = lax.broadcasted_iota(jnp.int32, (classes, LANES), 1)
    put(CYCLES, 0, jnp.where(lane < LANES // 2, mass_high, mass - mass_high))

    swaps, scatters, own_copies = [], [], []

    def give(lot, first, count):
        copy = pltpu.make_async_remote_copy(
            src_ref=work.at[first:first + count, chips * DEPTH:n * DEPTH], dst_ref=swapped[lot],
            send_sem=swap_send.at[lot], recv_sem=swap_recv.at[lot], device_id=other, device_id_type=MESH)
        copy.start()
        swaps.append(copy)

    def pass_on(lot, first, count):
        swaps[lot].wait_recv()
        for d in (*range(1, chips), 0):
            for j in range(count):
                both_cores = (work[first + j, d * DEPTH:(d + 1) * DEPTH, :]
                              + swapped[lot][j, d * DEPTH:(d + 1) * DEPTH, :])
                if d:
                    part[lot][d, :, j * LANES:(j + 1) * LANES] = both_cores.astype(jnp.bfloat16)
                else:
                    work[first + j, 0:DEPTH, :] = both_cores
            if d:
                copy = pltpu.make_async_remote_copy(
                    src_ref=part[lot].at[d], dst_ref=landed[lot].at[d], send_sem=send2.at[lot, d],
                    recv_sem=recv2.at[lot, d], device_id=behind(d), device_id_type=MESH)
                copy.start()
                scatters.append(copy)
        copy = pltpu.make_async_copy(
            work.at[first:first + count, 0:DEPTH], own_hbm.at[first:first + count], own_sem.at[lot])
        copy.start()
        own_copies.append(copy)

    lots_left = list(each(parts_out))
    given = []
    for c in range(CYCLES):
        if c % 2 == 0:
            mixed = jnp.dot(
                high, jnp.concatenate([shifted(c), shifted(c + 1)], axis=1), preferred_element_type=jnp.float32)
        at = c % 2 * ANGLES
        out = None
        for s in range(SHIFTS):
            piece = mixed[s * classes:(s + 1) * classes, at:at + ANGLES]
            if s:
                piece = pltpu.roll(piece, ANGLES - s * STEP, 1)
            out = piece if out is None else out + piece
        for b in range(TURNS):
            put(c, b, out[:, b * LANES:(b + 1) * LANES])
        if given and given[0][0] + 3 <= c:
            pass_on(*given.pop(0)[1])
        done = (c + 1) * TURNS * owned
        while lots_left and (done >= (lots_left[0][1] + lots_left[0][2]) * DEPTH or c == CYCLES - 1):
            give(*lots_left[0])
            given.append((c, lots_left.pop(0)))
    for _, lot in given:
        pass_on(*lot)

    for copies in gathers:
        for copy in copies.values():
            copy.wait_send()
    for copy in swaps:
        copy.wait_send()
    for copy in own_copies:
        copy.wait()
    evid_copy.wait()
    for copy in scatters:
        copy.wait()


def finish(owned, parts_out, *refs):
    lots = len(parts_out)
    landed, (own_hbm, evid_hbm, sums_ref, mass_ref, evid_ref) = refs[:lots], refs[lots:lots + 5]
    arrived, (work, evid, sems) = refs[lots + 5:-3], refs[-3:]
    loads = [pltpu.make_async_copy(src, dst, sems.at[i]) for i, (src, dst) in enumerate(
        zip((own_hbm, evid_hbm, *landed), (work, evid, *arrived)))]
    for load in loads:
        load.start()
    loads[0].wait()
    for lot, first, count in each(parts_out):
        loads[2 + lot].wait()
        for j in range(count):
            acc = work[first + j]
            for d in range(1, arrived[lot].shape[0]):
                acc = acc + arrived[lot][d, :, j * LANES:(j + 1) * LANES].astype(jnp.float32)
            work[first + j] = acc
    for c in range(CYCLES):
        for b in range(TURNS):
            at = (c * TURNS + b) * LANES
            for k in range(owned):
                j, row = spot(owned, c, b, k)
                sums_ref[k:k + 1, at:at + LANES] = work[j, row:row + 1, :]
    lane = lax.broadcasted_iota(jnp.int32, (1, LANES), 1)
    mass = jnp.zeros((1, LANES), jnp.float32)
    for k in range(owned):
        j, row = spot(owned, CYCLES, 0, k)
        tail = work[j, row:row + 1, :]
        mass = jnp.where(lane == k, tail + pltpu.roll(tail, LANES // 2, 1), mass)
    mass_ref[...] = mass[:, 0:owned]
    loads[1].wait()
    evid_ref[...] = evid[...]


def local(particles, references, inv_noise, assign):
    rows, width = particles.shape
    owned = references.shape[0]
    n = lax.axis_size("blk")
    chips = n // 2
    columns = -(-(CYCLES * TURNS + 1) * owned // DEPTH)
    parts_in = (columns - columns * 2 // 5, columns * 2 // 5)
    parts_out = (columns // 5,) * 3 + (columns - columns // 5 * 3,)
    vmem = pl.BlockSpec(memory_space=pltpu.VMEM)
    hbm = pl.BlockSpec(memory_space=pltpu.HBM)

    def slots(count, parts):
        return [pltpu.VMEM((count, DEPTH, part * LANES), jnp.bfloat16) for part in parts]

    shares = pl.pallas_call(
        functools.partial(kernel, n, owned, parts_in, parts_out),
        out_shape=(
            *(jax.ShapeDtypeStruct((chips, DEPTH, part * LANES), jnp.bfloat16) for part in parts_out),
            jax.ShapeDtypeStruct((columns, DEPTH, LANES), jnp.float32),
            jax.ShapeDtypeStruct((1, rows), jnp.float32),
        ),
        in_specs=[hbm] * 4,
        out_specs=(hbm,) * (len(parts_out) + 2),
        scratch_shapes=[
            pltpu.VMEM((rows, width), jnp.bfloat16),
            pltpu.VMEM((width, rows), jnp.bfloat16),
            pltpu.VMEM((owned, width), jnp.bfloat16),
            pltpu.VMEM((1, rows), jnp.float32),
            pltpu.VMEM((TOPK, rows), jnp.int32),
            pltpu.VMEM((1, rows), jnp.float32),
            pltpu.VMEM((columns, n * DEPTH, LANES), jnp.float32),
            *slots(n, parts_in),
            *(pltpu.VMEM((part, chips * DEPTH, LANES), jnp.float32) for part in parts_out),
            *slots(chips, parts_out),
            pltpu.SemaphoreType.DMA,
            pltpu.SemaphoreType.DMA((3,)),
            pltpu.SemaphoreType.DMA((len(parts_out),)),
            pltpu.SemaphoreType.DMA,
            pltpu.SemaphoreType.DMA((len(parts_in), n)),
            pltpu.SemaphoreType.DMA((len(parts_in), n)),
            pltpu.SemaphoreType.DMA((len(parts_out),)),
            pltpu.SemaphoreType.DMA((len(parts_out),)),
            pltpu.SemaphoreType.DMA((len(parts_out), chips)),
            pltpu.SemaphoreType.DMA((len(parts_out), chips)),
        ],
        compiler_params=pltpu.CompilerParams(
            collective_id=0, has_side_effects=True, vmem_limit_bytes=64 * 1024 * 1024 - 65536),
        cost_estimate=pl.CostEstimate(
            flops=6 * rows * n * owned * ROT * width, bytes_accessed=2 * rows * width, transcendentals=rows * n * owned * ROT),
    )(particles, references, inv_noise.reshape(1, rows), assign.T)
    sums, mass, evid = pl.pallas_call(
        functools.partial(finish, owned, parts_out),
        out_shape=(
            jax.ShapeDtypeStruct((owned, width), jnp.float32),
            jax.ShapeDtypeStruct((1, owned), jnp.float32),
            jax.ShapeDtypeStruct((1, rows), jnp.float32),
        ),
        in_specs=[hbm] * (len(parts_out) + 2),
        out_specs=(vmem, vmem, vmem),
        scratch_shapes=[
            *slots(chips, parts_out),
            pltpu.VMEM((columns, DEPTH, LANES), jnp.float32),
            pltpu.VMEM((1, rows), jnp.float32),
            pltpu.SemaphoreType.DMA((len(parts_out) + 2,)),
        ],
        compiler_params=pltpu.CompilerParams(vmem_limit_bytes=64 * 1024 * 1024 - 65536),
    )(*shares)
    return sums, mass.reshape(owned), evid.reshape(rows)


def solution(mesh):
    placed = (
        P(("parts", "blk"), None),
        P(("parts", "blk"), None),
        P(("parts", "blk")),
        P(("parts", "blk"), None),
    )
    return jax.shard_map(
        local,
        mesh=mesh,
        in_specs=placed,
        out_specs=(P(("parts", "blk"), None), P(("parts", "blk")), P(("parts", "blk"))),
        check_vma=False,
    )
```
